128 devices in a mesh: expert: 16 (over x, z_lo, core), tensor: 8 (over y, z_hi).
Axes of the slice: x: 4, y: 4, z: 4 (z_hi: 2, z_lo: 2; z = z_hi * 2 + z_lo), core: 2. Of those that a mesh axis runs over, the one named last changes fastest.
Arguments:
- tokens: bfloat16 [2048, 4096], P('expert', 'tensor'), may hold values from -6 to 6
- routes: int32 [2048, 8], P('expert'), may hold values from 0 to 63, all different within a row; in each aligned block of 128 rows (0 to 127, 128 to 255, ...) at most 32 rows name the same one
- gates: float32 [2048, 8], P('expert'), may hold values from 0.05 to 1
- w_gate: bfloat16 [64, 1536, 4096], P('expert', 'tensor'), may hold values from -0.09375 to 0.09375
- w_up: bfloat16 [64, 1536, 4096], P('expert', 'tensor'), may hold values from -0.09375 to 0.09375
- w_down: bfloat16 [64, 1536, 4096], P('expert', 'tensor'), may hold values from -0.15625 to 0.15625
Outputs:
- combined: bfloat16 [2048, 4096], P('expert', 'tensor')
The draws below stay inside these ranges and needn't reach their ends.
Inputs may be any that keep to these rules, and one draw needn't show every extreme that they name: `routes`: each row names 8 different experts; within the rows of one device (aligned blocks of 128 rows) no expert is named by more than 32 rows, a bound that some block reaches.
All inputs are finite; a program needn't handle non-finite values.
Results may differ from the reference program's by a relative error of at most 0.018.
Values may be sent and summed in bfloat16 or wider, within the bound.
No kernel may reach another device: no remote copies, remote signals or barrier semaphores. Data moves between devices by JAX's collectives and lax.ppermute only.
A program may use at most 192 MiB of HBM per device.

```python
import math
import jax
import jax.numpy as jnp
import numpy as np
from jax import lax

D = 4096
FF = 1536
TOPK = 8
TOK_DEV = 128
EXPERTS = 64
TOKENS = 2048
CAP = 32
N_EXPERT = 16
N_TENSOR = 8


def levels(key, shape, pieces, low, high):
    level, own = 1.0, jax.random.fold_in(key, 6)
    for axis_at, parts in pieces:
        heights = jnp.exp(jax.random.uniform(jax.random.fold_in(own, axis_at), (parts,), jnp.float32, low / len(pieces), high / len(pieces)))
        level = level * jnp.repeat(heights, shape[axis_at] // parts).reshape([-1 if axis == axis_at else 1 for axis in range(len(shape))])
    return level


def assign_block(rng, own, number, rows, count, top, bound, skew):
    ranking = jax.random.permutation(rng, count)
    packed, common = load_shares(count, rows * top, bound, skew, True), load_shares(count, rows * top, bound, skew, False)
    places = jnp.arange(count)

    def named(tallies, offset_by):
        used = int((tallies > 0).sum())
        fixed = max(1, used // 4)
        moved = fixed + (places - fixed + offset_by * (used - fixed)) % max(1, count - fixed)
        return jnp.zeros((count,), jnp.int32).at[ranking[jnp.where(places < fixed, places, moved)]].set(jnp.asarray(tallies, jnp.int32))

    tallies = jnp.where(number % 4 == 0, named(packed, number // 4), named(common, number - number // 4 - 1))
    mixed = jax.random.permutation(jax.random.fold_in(own, 3), count)
    giver, sink = mixed[0:count // 2 * 2:2], mixed[1:count // 2 * 2:2]
    margin = jnp.minimum(tallies[giver] - 1, bound - tallies[sink]) // 2
    margin = jnp.where((giver == ranking[0]) | (sink == ranking[0]) | (tallies[sink] == 0), 0, jnp.maximum(margin, 0))
    moved = jax.random.randint(jax.random.fold_in(own, 4), (count // 2,), 0, 1 << 20) % (margin + 1)
    tallies = tallies.at[giver].add(-moved).at[sink].add(moved)
    items = jnp.searchsorted(jnp.cumsum(tallies), jnp.arange(rows * top), side="right").astype(jnp.int32)
    table = items.reshape(top, rows).T
    table = table[jax.random.permutation(jax.random.fold_in(own, 1), rows)]
    offset_by = jax.random.randint(jax.random.fold_in(own, 2), (rows, 1), 0, top)
    return jnp.take_along_axis(table, (jnp.arange(top)[None, :] + offset_by) % top, axis=1)


def load_shares(number_of, total, reach, skew, full):
    portions = [(1 << 20) // math.isqrt(rank ** skew) + 1 for rank in range(1, number_of + 1)]
    largest = reach if full else min(reach, max(-(-total // number_of), total * portions[0] // sum(portions)))
    least = 1 if total - largest >= number_of - 1 else 0
    holding, rest = [largest] + [least] * (number_of - 1), total - largest - least * (number_of - 1)
    while rest > 0:
        movable = [i for i in range(1, number_of) if holding[i] < largest] or [i for i in range(1, number_of) if holding[i] < reach]
        pool, budget = sum([portions[i] for i in movable]), rest
        for i in movable:
            more = min(reach - holding[i], max(1, budget * portions[i] // pool), rest)
            holding[i] = holding[i] + more
            rest = rest - more
    return np.array(holding)


def normal_values(stream_key, dims, scale, reach, shards=(), held_as=jnp.bfloat16):
    factor_of = levels(stream_key, dims, shards, -0.22, 0.18) if shards else 1.0
    array = jax.random.normal(stream_key, dims, jnp.float32) * scale * factor_of
    return jnp.minimum(jnp.maximum(array, -reach), reach).astype(held_as)


def setup_inputs(seed: int = 0) -> dict:
    key_list = jax.random.split(jax.random.key(seed), 7)
    tokens = normal_values(key_list[0], (TOKENS, D), 1.0, 6.0, ((0, 16), (1, 8)))
    routes_keys = jax.random.split(jax.random.fold_in(key_list[1], 1), TOKENS // TOK_DEV)
    routes_turns = jax.random.permutation(jax.random.fold_in(key_list[1], 3), TOKENS // TOK_DEV)
    routes = jax.vmap(lambda own, number: assign_block(jax.random.fold_in(key_list[1], 2), own, number, TOK_DEV, EXPERTS, TOPK, CAP, 2))(routes_keys, routes_turns).reshape((TOKENS, TOPK))
    gates = jnp.clip(jnp.exp(math.log(1.0) - 2.9957323 * jax.random.uniform(key_list[2], (TOKENS, TOPK), jnp.float32) ** levels(key_list[2], (TOKENS, TOPK), ((0, 16),), -0.2, 0.2)), 0.05, 1.0)
    w_gate = normal_values(key_list[3], (EXPERTS, FF, D), D ** -0.5, 0.09375, ((0, 16), (1, 8)))
    w_up = normal_values(key_list[4], (EXPERTS, FF, D), D ** -0.5, 0.09375, ((0, 16), (1, 8)))
    w_down = normal_values(key_list[5], (EXPERTS, FF, D), FF ** -0.5, 0.15625, ((0, 16), (1, 8)))
    return {"tokens": tokens, "routes": routes, "gates": gates, "w_gate": w_gate, "w_up": w_up, "w_down": w_down}


def reference(tokens, routes, gates, w_gate, w_up, w_down):
    flat_routes = routes.reshape(N_EXPERT, TOK_DEV * TOPK)
    onehot = (flat_routes[:, :, None] == jnp.arange(EXPERTS, dtype=jnp.int32)[None, None, :]).astype(jnp.int32)
    before = jnp.cumsum(onehot, axis=1) - onehot
    slot_index = jnp.sum(before * onehot, axis=2).reshape(-1).astype(jnp.int32)
    source = (jnp.arange(TOKENS * TOPK, dtype=jnp.int32) // (TOK_DEV * TOPK)).astype(jnp.int32)
    target = ((routes.reshape(-1) * N_EXPERT + source) * CAP + slot_index).astype(jnp.int32)
    token_rows = jnp.repeat(tokens, TOPK, axis=0)
    buffer = jnp.zeros((EXPERTS * N_EXPERT * CAP, D), jnp.bfloat16).at[target].set(token_rows)
    buffer = buffer.reshape(EXPERTS, N_EXPERT * CAP, D)

    def one_expert(operands):
        rows_in, gate_mat, up_mat, down_mat = operands
        gate_act = jnp.dot(rows_in, gate_mat.T, preferred_element_type=jnp.float32)
        up_act = jnp.dot(rows_in, up_mat.T, preferred_element_type=jnp.float32)
        hidden = (jax.nn.silu(gate_act) * up_act).astype(jnp.bfloat16)
        grouped = hidden.reshape(N_EXPERT * CAP, N_TENSOR, FF // N_TENSOR).astype(jnp.float32)
        down_groups = down_mat.reshape(N_TENSOR, FF // N_TENSOR, D).astype(jnp.float32)
        partials = jnp.einsum("rgf,gfd->grd", grouped, down_groups).astype(jnp.bfloat16)
        return jnp.sum(partials.astype(jnp.float32), axis=0)

    expert_out = lax.map(one_expert, (buffer, w_gate, w_up, w_down))
    picked = expert_out.reshape(-1, D)[target].reshape(TOKENS, TOPK, D)
    combined = jnp.sum(gates[:, :, None] * picked, axis=1)
    return combined.astype(jnp.bfloat16)
```

```python
import functools

import jax
import jax.numpy as jnp
from jax import lax
from jax.experimental import pallas as pl
from jax.experimental.pallas import tpu as pltpu
from jax.sharding import PartitionSpec as P

AXES = ("expert", "tensor")
ROWS = (48, 48, 32)
FIRST = (0, 48, 96)
BF16 = jnp.bfloat16
F32 = jnp.float32


def device_number(x, y, z, core):
    return (x * 4 + (z % 2) * 2 + core) * 8 + y * 2 + z // 2


def places():
    return [(x, y, z, c) for x in range(4) for y in range(4) for z in range(4) for c in range(2)]


def ring_pairs(dim, sub):
    pairs = []
    for place in places():
        other = list(place)
        other[dim] ^= 1 if sub == place[3] else 3
        pairs.append((device_number(*place), device_number(*other)))
    return pairs


def core_pairs():
    return [(device_number(x, y, z, c), device_number(x, y, z, 1 - c)) for x, y, z, c in places()]


def swap(value, dim, sub):
    return lax.ppermute(value, AXES, ring_pairs(dim, sub))


def gather_tokens(tokens):
    parts = [tokens[first : first + rows][None] for first, rows in zip(FIRST, ROWS)]
    for phase in (0, 1):
        for sub in (0, 1):
            got = [swap(part, (i + phase) % 3, sub) for i, part in enumerate(parts)]
            parts = [jnp.concatenate([part, new], 0) for part, new in zip(parts, got)]
    one = [swap(part, (i + 2) % 3, 0) for i, part in enumerate(parts)]
    two = [swap(part, (i + 2) % 3, 1) for i, part in enumerate(parts)]
    three = [swap(part, (i + 2) % 3, 1) for i, part in enumerate(one)]
    return [list(pieces) for pieces in zip(parts, one, two, three)]


def scatter_sums(parts):
    far = [swap(p[2], (i + 2) % 3, 1) for i, p in enumerate(parts)]
    side = [swap(p[3], (i + 2) % 3, 1) for i, p in enumerate(parts)]
    near = [p[1] + s for p, s in zip(parts, side)]
    got = [swap(p, (i + 2) % 3, 0) for i, p in enumerate(near)]
    held = [p[0] + s + r for p, s, r in zip(parts, far, got)]
    for phase in (1, 0):
        for sub in (1, 0):
            half = held[0].shape[0] // 2
            got = [swap(p[half:], (i + phase) % 3, sub) for i, p in enumerate(held)]
            held = [p[:half] + r for p, r in zip(held, got)]
    return jnp.concatenate([p[0] for p in held], 0)


def z_place(low, high, core):
    if low == 0:
        return 3 * high
    return 1 + (high ^ core)


def x_copies(sc_ref, x_refs, x_all, sem):
    core = sc_ref[8]
    copies = []

    def column(ky, kz):
        if kz == 0 or kz == 3:
            f = sc_ref[ky * 2 + kz // 3]
        else:
            f = sc_ref[ky * 2 + ((kz - 1) ^ core)]
        return pl.ds(pl.multiple_of(f * 512, 512), 512)

    for i in range(3):
        rows = pl.ds(FIRST[i], ROWS[i])
        for k3 in range(4):
            src = x_refs[i * 4 + k3]
            for k in range(4):
                if i == 0:
                    kz, ky = k3, k
                    low = (0, 1, 1, 0)[kz]
                    copies.append((src.at[ky], x_all.at[:, low, rows, column(ky, kz)]))
                elif i == 1:
                    kx, kz = k3, k
                    low = (0, 1, 1, 0)[kz]
                    for ky in range(4):
                        copies.append((src.at[kz, ky], x_all.at[kx, low, rows, column(ky, kz)]))
                else:
                    ky, kz = k3, k
                    low = (0, 1, 1, 0)[kz]
                    copies.append((src.at[:, kz], x_all.at[:, low, rows, column(ky, kz)]))
    return [pltpu.make_async_copy(a, b, sem.at[n]) for n, (a, b) in enumerate(copies)]


N_X_COPIES = 96


def hidden_kernel(sc_ref, p_ref, q_ref, gs_ref, wg, wu, wg2, wu2, *rest):
    x_refs = rest[:12]
    hd_ref, x_all, xd, wbuf, hp, x_sem, w_sem = rest[12:]

    def fetch(pair, j, gate, up):
        e = lax.rem(pair, 2) * 2 + j
        return [
            pltpu.make_async_copy(gate.at[e], wbuf.at[j, pl.ds(0, 192)], w_sem.at[j, 0]),
            pltpu.make_async_copy(up.at[e], wbuf.at[j, pl.ds(192, 192)], w_sem.at[j, 1]),
        ]

    x_in = x_copies(sc_ref, x_refs, x_all, x_sem)
    for copy in x_in:
        copy.start()
    for j in range(2):
        for copy in fetch(0, j, wg, wu):
            copy.start()
    hp[...] = jnp.zeros_like(hp)
    for copy in x_in:
        copy.wait()

    def dispatch(n, carry):
        b = n // 8
        col = pl.ds(pl.multiple_of(lax.rem(n, 8) * 512, 512), 512)
        rows = jnp.dot(p_ref[b], x_all[b // 2, lax.rem(b, 2), :, col], preferred_element_type=F32)
        xd[:, pl.ds(pl.multiple_of(b * 32, 32), 32), col] = rows.astype(BF16).reshape(8, 32, 512)
        return carry

    lax.fori_loop(0, 64, dispatch, 0)

    def experts(pair, carry):
        for j in range(2):
            e = pair * 2 + j
            for copy in fetch(pair, j, wg, wu):
                copy.wait()
            act = lax.dot_general(
                wbuf[j], xd[e], (((1,), (1,)), ((), ())), preferred_element_type=F32
            )
            gate, up = act[:192], act[192:]
            hidden = gate / (1.0 + jnp.exp(-gate)) * up * gs_ref[e]
            hp[pl.ds(j * 192, 192), pl.ds(j * 256, 256)] = hidden.astype(BF16)

            @pl.when(pair == 0)
            def _():
                for copy in fetch(pair + 1, j, wg, wu):
                    copy.start()

            @pl.when((pair == 1) | (pair == 2))
            def _():
                for copy in fetch(pair + 1, j, wg2, wu2):
                    copy.start()

        def spread(r, c2):
            rows = pl.ds(pl.multiple_of(r * 256, 256), 256)
            out = lax.dot_general(
                q_ref[rows, pl.ds(pl.multiple_of(pair * 512, 512), 512)],
                hp[...],
                (((1,), (1,)), ((), ())),
                preferred_element_type=F32,
            )
            hd_ref[rows, pl.ds(pl.multiple_of(pair * 384, 128), 384)] = out.astype(BF16)
            return c2

        lax.fori_loop(0, 4, spread, 0)
        return carry

    lax.fori_loop(0, 4, experts, 0)


def down_kernel(sc_ref, hd_ref, wd, wd2, *rest):
    outs = rest[:12]
    wbuf, ybuf, w_sem, y_sem = rest[12:]
    core = sc_ref[8]

    def fetch(f):
        slot = f % 2
        col = pl.ds(pl.multiple_of(sc_ref[f] * 512, 512), 512)
        return [
            pltpu.make_async_copy(wd.at[:, :, col], wbuf.at[slot, pl.ds(0, 4)], w_sem.at[slot, 0]),
            pltpu.make_async_copy(wd2.at[:, :, col], wbuf.at[slot, pl.ds(4, 4)], w_sem.at[slot, 1]),
        ]

    def stores(f, turn):
        slot, ky, high = f % 2, f // 2, f % 2
        y = ybuf.at[slot]
        copies = []
        for low in range(2):
            kz = z_place(low, high, turn if turn is not None else core)
            rows = [pl.ds(FIRST[i], ROWS[i]) for i in range(3)]
            if turn is not None and low == 1:
                copies.append((y.at[:, low, rows[0]], outs[kz].at[ky]))
            if turn is None:
                if low == 0:
                    copies.append((y.at[:, low, rows[0]], outs[kz].at[ky]))
                for kx in range(4):
                    copies.append((y.at[kx, low, rows[1]], outs[4 + kx].at[kz, ky]))
                copies.append((y.at[:, low, rows[2]], outs[8 + ky].at[:, kz]))
        first = 0 if turn is None else 11
        return [
            pltpu.make_async_copy(a, b, y_sem.at[slot, first + n]) for n, (a, b) in enumerate(copies)
        ]

    for copy in fetch(0) + fetch(1):
        copy.start()
    for f in range(8):
        slot = f % 2
        for copy in fetch(f):
            copy.wait()
        if f >= 2:
            for copy in stores(f - 2, None) + stores(f - 2, 0):
                copy.wait()

        def rows_step(kx, carry):
            rows = pl.ds(pl.multiple_of(kx * 256, 256), 256)
            out = jnp.dot(
                hd_ref[rows], wbuf[slot].reshape(1536, 512), preferred_element_type=F32
            )
            ybuf[slot, kx] = out.astype(BF16).reshape(2, 128, 512)
            return carry

        lax.fori_loop(0, 4, rows_step, 0)
        if f < 6:
            for copy in fetch(f + 2):
                copy.start()
        for copy in stores(f, None):
            copy.start()
        for turn in range(2):

            @pl.when(core == turn)
            def _():
                for copy in stores(f, turn):
                    copy.start()

    for f in (6, 7):
        for copy in stores(f, None) + stores(f, 0):
            copy.wait()


def local(tokens, routes, gates, w_gate, w_up, w_down):
    e, t = lax.axis_index("expert"), lax.axis_index("tensor")
    x, zlo, core, y, zhi = e // 4, e // 2 % 2, e % 2, t // 2, t % 2
    offs = [0, jnp.where(core == 0, 1, 3), jnp.where(core == 0, 3, 1), 2]

    wg2, wu2, wd2 = [lax.ppermute(w, AXES, core_pairs()) for w in (w_gate, w_up, w_down)]

    packed = jnp.concatenate([routes.astype(F32), gates], axis=1)
    spread = lax.all_gather(packed, "expert")
    blocks = jnp.stack(
        [(x ^ offs[kx]) * 4 + (zlo ^ low) * 2 + core for kx in range(4) for low in range(2)]
    )
    mine = jnp.take(spread, blocks, axis=0)
    ids = jnp.concatenate([e * 4 + jnp.arange(4), (e ^ 1) * 4 + jnp.arange(4)]).astype(F32)
    hit = mine[:, :, None, :8] == ids[None, None, :, None]
    named = jnp.any(hit, axis=3).astype(BF16)
    weight = jnp.sum(jnp.where(hit, mine[:, :, None, 8:], 0.0), axis=3)
    earlier = (jnp.arange(128)[:, None] < jnp.arange(128)[None, :]).astype(BF16)
    slot = jnp.einsum("bte,ts->bse", named, earlier, preferred_element_type=F32)
    slot = jnp.where(named > 0, slot, -1.0)
    slots = jnp.arange(32, dtype=F32)
    chosen = jnp.swapaxes(slot, 1, 2)[:, :, None, :] == slots[None, None, :, None]
    p_mat = chosen.astype(BF16).reshape(8, 256, 128)
    gslot = jnp.sum(jnp.where(chosen, jnp.swapaxes(weight, 1, 2)[:, :, None, :], 0.0), axis=3)
    gslot = jnp.swapaxes(gslot, 0, 1).reshape(8, 1, 256)
    wide = jnp.arange(256)
    q_mat = (slot[..., None] == (wide % 32).astype(F32)) & (
        wide // 32 == jnp.arange(8)[:, None, None, None]
    )
    q_mat = q_mat.astype(BF16).reshape(1024, 2048)

    scalars = jnp.stack(
        [(y ^ offs[ky]) * 2 + (zhi ^ high) for ky in range(4) for high in range(2)] + [core]
    ).astype(jnp.int32)

    parts = gather_tokens(tokens)
    pieces = [
        piece.reshape(4, 4, ROWS[i], 512) for i, part in enumerate(parts) for piece in part
    ]
    smem = pl.BlockSpec(memory_space=pltpu.SMEM)
    vmem = pl.BlockSpec(memory_space=pltpu.VMEM)
    hbm = pl.BlockSpec(memory_space=pl.ANY)
    hidden = pl.pallas_call(
        hidden_kernel,
        out_shape=jax.ShapeDtypeStruct((1024, 1536), BF16),
        in_specs=[smem, vmem, vmem, vmem] + [hbm] * 16,
        out_specs=vmem,
        scratch_shapes=[
            pltpu.VMEM((4, 2, 128, 4096), BF16),
            pltpu.VMEM((8, 256, 4096), BF16),
            pltpu.VMEM((2, 384, 4096), BF16),
            pltpu.VMEM((384, 512), BF16),
            pltpu.SemaphoreType.DMA((N_X_COPIES,)),
            pltpu.SemaphoreType.DMA((2, 2)),
        ],
        compiler_params=pltpu.CompilerParams(vmem_limit_bytes=56 * 2**20),
        name="hidden",
    )(scalars, p_mat, q_mat, gslot, w_gate, w_up, wg2, wu2, *pieces)

    sums = pl.pallas_call(
        down_kernel,
        out_shape=[
            jax.ShapeDtypeStruct((4, 4, ROWS[i], 512), BF16) for i in range(3) for _ in range(4)
        ],
        in_specs=[smem, vmem, hbm, hbm],
        out_specs=[hbm] * 12,
        scratch_shapes=[
            pltpu.VMEM((2, 8, 192, 512), BF16),
            pltpu.VMEM((2, 4, 2, 128, 512), BF16),
            pltpu.SemaphoreType.DMA((2, 2)),
            pltpu.SemaphoreType.DMA((2, 12)),
        ],
        compiler_params=pltpu.CompilerParams(vmem_limit_bytes=56 * 2**20),
        name="down",
    )(scalars, hidden, w_down, wd2)
    parts = [
        [sums[i * 4 + k].reshape(16, ROWS[i], 512) for k in range(4)] for i in range(3)
    ]
    return scatter_sums(parts)


def solution(mesh):
    placed = (
        P("expert", "tensor"),
        P("expert", None),
        P("expert", None),
        P("expert", "tensor", None),
        P("expert", "tensor", None),
        P("expert", "tensor", None),
    )
    return jax.shard_map(
        local, mesh=mesh, in_specs=placed, out_specs=P("expert", "tensor"), check_vma=False
    )
```

```python
import jax
import jax.numpy as jnp
from jax import lax
from jax.experimental import pallas as pl
from jax.experimental.pallas import tpu as pltpu
from jax.sharding import PartitionSpec as P

AXES = ("expert", "tensor")
OFF = (0, 1, 3, 2)
LOW = (0, 1, 1, 0)
HIGH = (0, 0, 1, 1)
ROWS = (48, 48, 32)
FIRST = (0, 48, 96)
BF16 = jnp.bfloat16
F32 = jnp.float32


def device_number(x, y, z, core):
    return (x * 4 + (z % 2) * 2 + core) * 8 + y * 2 + z // 2


def places():
    return [(x, y, z, c) for x in range(4) for y in range(4) for z in range(4) for c in range(2)]


def swap(value, dim, mask):
    pairs = []
    for place in places():
        other = list(place)
        other[dim] ^= mask
        pairs.append((device_number(*place), device_number(*other)))
    return lax.ppermute(value, AXES, pairs)


def from_other_core(value):
    pairs = [(device_number(x, y, z, c), device_number(x, y, z, 1 - c)) for x, y, z, c in places()]
    return lax.ppermute(value, AXES, pairs)


def swap_each(parts, phase, mask):
    return [swap(part, (i + phase) % 3, mask) for i, part in enumerate(parts)]


def double(parts, phase, mask):
    got = swap_each(parts, phase, mask)
    return [jnp.concatenate([part, new], 0) for part, new in zip(parts, got)]


def gather_last(parts):
    one = swap_each(parts, 2, 1)
    three = swap_each(parts, 2, 3)
    two_a = swap_each([p[:8] for p in one], 2, 3)
    two_b = swap_each([p[8:] for p in three], 2, 1)
    return list(zip(parts, one, three, two_a, two_b))


def scatter_sums(parts):
    own, one, three, two_a, two_b = (list(p) for p in zip(*parts))
    got_a = swap_each(two_a, 2, 3)
    got_b = swap_each(two_b, 2, 1)
    one = [jnp.concatenate([p[:8] + g, p[8:]], 0) for p, g in zip(one, got_a)]
    three = [jnp.concatenate([p[:8], p[8:] + g], 0) for p, g in zip(three, got_b)]
    got_a = swap_each(one, 2, 1)
    got_b = swap_each(three, 2, 3)
    held = [
        (p.astype(F32) + a.astype(F32) + b.astype(F32)).astype(BF16)
        for p, a, b in zip(own, got_a, got_b)
    ]
    for phase in (1, 0):
        for mask in (3, 1):
            half = held[0].shape[0] // 2
            got = swap_each([p[half:] for p in held], phase, mask)
            held = [p[:half] + r for p, r in zip(held, got)]
    return jnp.concatenate([p[0] for p in held], 0)


def piece(refs, i, k3, k2, k1):
    group = refs[i * 5 : i * 5 + 5]
    if k3 < 3:
        return [group[k3].at[slice(None) if k2 is None else k2, slice(None) if k1 is None else k1]]
    if k2 is None:
        return [half.at[:, k1] for half in group[3:]]
    return [group[3 + k2 // 2].at[k2 % 2, slice(None) if k1 is None else k1]]


def place_of(low, high):
    return [k for k in range(4) if (LOW[k], HIGH[k]) == (low, high)][0]


def block_pieces(refs, tile, column):
    def pairs(ky, kz):
        found = []
        low, cols = LOW[kz], column(ky, kz)
        rows = [pl.ds(first, count) for first, count in zip(FIRST, ROWS)]
        (hbm,) = piece(refs, 0, kz, ky, None)
        found.append((hbm, tile.at[:, low, rows[0], cols]))
        for kx in range(4):
            (hbm,) = piece(refs, 1, kx, kz, ky)
            found.append((hbm, tile.at[kx, low, rows[1], cols]))
        halves = piece(refs, 2, ky, None, kz)
        for n, hbm in enumerate(halves):
            step = 4 // len(halves)
            found.append((hbm, tile.at[pl.ds(n * step, step), low, rows[2], cols]))
        return found

    return pairs


def route(ids_ref, mine_ref, slot_ref, gate_col, pick):
    before = lax.broadcasted_iota(jnp.int32, (128, 128), 0)
    before = (before < lax.broadcasted_iota(jnp.int32, (128, 128), 1)).astype(BF16)
    number = lax.broadcasted_iota(jnp.int32, (8, 32, 128), 1).astype(F32)
    line = lax.broadcasted_iota(jnp.int32, (8, 128), 0)

    def block(b, carry):
        named = jnp.zeros((8, 128), F32)
        weight = jnp.zeros((8, 128), F32)
        for e in range(8):
            hit = mine_ref[b, 0:8] == ids_ref[e]
            any_hit = jnp.max(jnp.where(hit, 1.0, 0.0), axis=0, keepdims=True)
            gate = jnp.sum(jnp.where(hit, mine_ref[b, 8:16], 0.0), axis=0, keepdims=True)
            named = jnp.where(line == e, any_hit, named)
            weight = jnp.where(line == e, gate, weight)
        slot = jnp.dot(named.astype(BF16), before, preferred_element_type=F32)
        slot = jnp.where(named > 0, slot, -1.0)
        slot_ref[b] = slot
        chosen = slot[:, None, :] == number
        pick[b] = jnp.where(chosen, 1.0, 0.0).astype(BF16).reshape(256, 128)
        rows = pl.ds(pl.multiple_of(b * 32, 32), 32)
        gate_col[:, rows, :] = jnp.sum(
            jnp.where(chosen, weight[:, None, :], 0.0), axis=2, keepdims=True
        )
        return carry

    lax.fori_loop(0, 8, block, 0)


N_TOKEN_COPIES = 100


def hidden_kernel(ids_ref, cols_ref, mine_ref, wg, wu, wg2, wu2, *rest):
    token_refs = rest[:15]
    h_ref, slot_ref, tokens, sorted_rows, wbuf, gate_col, pick, t_sem, w_sem = rest[15:]

    def fetch(e, j, gate, up):
        return [
            pltpu.make_async_copy(gate.at[e], wbuf.at[j, pl.ds(0, 192)], w_sem.at[j, 0]),
            pltpu.make_async_copy(up.at[e], wbuf.at[j, pl.ds(192, 192)], w_sem.at[j, 1]),
        ]

    def column(ky, kz):
        return pl.ds(pl.multiple_of(cols_ref[ky * 2 + HIGH[kz]] * 512, 512), 512)

    pairs = block_pieces(token_refs, tokens, column)
    loads = [pair for ky in range(4) for kz in range(4) for pair in pairs(ky, kz)]
    loads = [pltpu.make_async_copy(a, b, t_sem.at[n]) for n, (a, b) in enumerate(loads)]
    for copy in loads:
        copy.start()
    route(ids_ref, mine_ref, slot_ref, gate_col, pick)
    for copy in loads:
        copy.wait()
    for j in range(4):
        for copy in fetch(j, j, wg, wu):
            copy.start()

    def dispatch(b, carry):
        rows = jnp.dot(pick[b], tokens[b // 2, lax.rem(b, 2)], preferred_element_type=F32)
        sorted_rows[:, pl.ds(pl.multiple_of(b * 32, 32), 32)] = rows.astype(BF16).reshape(
            8, 32, 4096
        )
        return carry

    lax.fori_loop(0, 8, dispatch, 0)

    def experts(turn, carry):
        for j in range(4):
            e = turn * 4 + j
            for copy in fetch(j, j, wg, wu):
                copy.wait()
            act = lax.dot_general(
                sorted_rows[e], wbuf[j], (((1,), (1,)), ((), ())), preferred_element_type=F32
            )
            gate, up = act[:, :192], act[:, 192:]
            hidden = gate / (1.0 + jnp.exp(-gate)) * up * gate_col[e]
            h_ref[e] = hidden.astype(BF16)

            @pl.when(turn == 0)
            def _():
                for copy in fetch(j, j, wg2, wu2):
                    copy.start()

        return carry

    lax.fori_loop(0, 2, experts, 0)


def down_kernel(cols_ref, h_ref, slot_ref, wd, wd2, *rest):
    outs = rest[:15]
    wbuf, expert_rows, ybuf, put, w_sem, y_sem = rest[15:]

    def fetch(ky):
        slot = ky % 2
        col = pl.ds(pl.multiple_of(cols_ref[ky * 2] // 2 * 1024, 1024), 1024)
        return [
            pltpu.make_async_copy(wd.at[:, :, col], wbuf.at[slot, pl.ds(0, 4)], w_sem.at[slot, 0]),
            pltpu.make_async_copy(wd2.at[:, :, col], wbuf.at[slot, pl.ds(4, 4)], w_sem.at[slot, 1]),
        ]

    def stores(ky):
        def column(ky, kz):
            side = lax.rem(cols_ref[ky * 2 + HIGH[kz]], 2)
            return pl.ds(pl.multiple_of(side * 512, 512), 512)

        pairs = block_pieces(outs, ybuf.at[ky % 2], column)
        found = [pair for kz in range(4) for pair in pairs(ky, kz)]
        return [
            pltpu.make_async_copy(b, a, y_sem.at[ky % 2, n]) for n, (a, b) in enumerate(found)
        ]

    for copy in fetch(0) + fetch(1):
        copy.start()
    number = lax.broadcasted_iota(jnp.int32, (8, 32, 128), 1).astype(F32)
    for b in range(8):
        chosen = jnp.where(slot_ref[b][:, None, :] == number, 1.0, 0.0).reshape(256, 128)
        put[b] = chosen.T.astype(BF16)
    for ky in range(4):
        slot = ky % 2
        for copy in fetch(ky):
            copy.wait()

        def project(e, carry):
            out = jnp.dot(h_ref[e], wbuf[slot, e], preferred_element_type=F32)
            rows = pl.ds(pl.multiple_of(e * 32, 32), 32)
            expert_rows[:, rows] = out.astype(BF16).reshape(8, 32, 1024)
            return carry

        lax.fori_loop(0, 8, project, 0, unroll=2)
        if ky < 2:
            for copy in fetch(ky + 2):
                copy.start()
        if ky >= 2:
            for copy in stores(ky - 2):
                copy.wait()

        def combine(b, carry):
            out = jnp.dot(put[b], expert_rows[b], preferred_element_type=F32)
            ybuf[slot, b // 2, lax.rem(b, 2)] = out.astype(BF16)
            return carry

        lax.fori_loop(0, 8, combine, 0, unroll=2)
        for copy in stores(ky):
            copy.start()
    for ky in (2, 3):
        for copy in stores(ky):
            copy.wait()


def local(tokens, routes, gates, w_gate, w_up, w_down):
    e, t = lax.axis_index("expert"), lax.axis_index("tensor")
    y, zhi = t // 2, t % 2
    ids = jnp.concatenate([e * 4 + jnp.arange(4), (e ^ 1) * 4 + jnp.arange(4)]).astype(F32)
    cols = jnp.stack([(y ^ OFF[ky]) * 2 + (zhi ^ high) for ky in range(4) for high in range(2)])
    cols = cols.astype(jnp.int32)

    packed = jnp.concatenate([routes.astype(F32), gates], axis=1).T[None]
    parts = [tokens[first : first + rows][None] for first, rows in zip(FIRST, ROWS)]

    wg2 = from_other_core(w_gate)
    for mask in (1, 3):
        parts = double(parts, 0, mask)
        packed = jnp.concatenate([packed, swap(packed, 0, mask)], 0)
    parts, wg2, w_up = lax.optimization_barrier((parts, wg2, w_up))
    wu2 = from_other_core(w_up)
    mine = jnp.stack([packed, swap(packed, 2, 1)], 1).reshape(8, 16, 128)
    for mask in (1, 3):
        parts = double(parts, 1, mask)
    parts, wu2, mine = lax.optimization_barrier((parts, wu2, mine))
    parts = gather_last(parts)
    parts, w_down = lax.optimization_barrier((parts, w_down))
    wd2 = from_other_core(w_down)
    pieces = [
        p.reshape(p.shape[0] // 4, 4, ROWS[i], 512) for i, part in enumerate(parts) for p in part
    ]
    smem = pl.BlockSpec(memory_space=pltpu.SMEM)
    vmem = pl.BlockSpec(memory_space=pltpu.VMEM)
    hbm = pl.BlockSpec(memory_space=pl.ANY)
    hidden, slots = pl.pallas_call(
        hidden_kernel,
        out_shape=[
            jax.ShapeDtypeStruct((8, 256, 192), BF16),
            jax.ShapeDtypeStruct((8, 8, 128), F32),
        ],
        in_specs=[smem, smem, vmem] + [hbm] * 19,
        out_specs=[vmem, vmem],
        scratch_shapes=[
            pltpu.VMEM((4, 2, 128, 4096), BF16),
            pltpu.VMEM((8, 256, 4096), BF16),
            pltpu.VMEM((4, 384, 4096), BF16),
            pltpu.VMEM((8, 256, 1), F32),
            pltpu.VMEM((8, 256, 128), BF16),
            pltpu.SemaphoreType.DMA((N_TOKEN_COPIES,)),
            pltpu.SemaphoreType.DMA((4, 2)),
        ],
        compiler_params=pltpu.CompilerParams(vmem_limit_bytes=56 * 2**20),
        name="hidden",
    )(ids, cols, mine, w_gate, w_up, wg2, wu2, *pieces)

    sums = pl.pallas_call(
        down_kernel,
        out_shape=[
            jax.ShapeDtypeStruct((4 if k < 3 else 2, 4, ROWS[i], 512), BF16)
            for i in range(3)
            for k in range(5)
        ],
        in_specs=[smem, vmem, vmem, hbm, hbm],
        out_specs=[hbm] * 15,
        scratch_shapes=[
            pltpu.VMEM((2, 8, 192, 1024), BF16),
            pltpu.VMEM((8, 256, 1024), BF16),
            pltpu.VMEM((2, 4, 2, 128, 1024), BF16),
            pltpu.VMEM((8, 128, 256), BF16),
            pltpu.SemaphoreType.DMA((2, 2)),
            pltpu.SemaphoreType.DMA((2, 28)),
        ],
        compiler_params=pltpu.CompilerParams(vmem_limit_bytes=56 * 2**20),
        name="down",
    )(cols, hidden, slots, w_down, wd2)
    parts = [
        [p.reshape(-1, ROWS[i], 512) for p in sums[i * 5 : i * 5 + 5]] for i in range(3)
    ]
    return scatter_sums(parts)


def solution(mesh):
    placed = (
        P("expert", "tensor"),
        P("expert", None),
        P("expert", None),
        P("expert", "tensor", None),
        P("expert", "tensor", None),
        P("expert", "tensor", None),
    )
    return jax.shard_map(
        local, mesh=mesh, in_specs=placed, out_specs=P("expert", "tensor"), check_vma=False
    )
```

```python
import functools

import jax
import jax.numpy as jnp
from jax import lax
from jax.experimental import pallas as pl
from jax.experimental.pallas import tpu as pltpu
from jax.sharding import PartitionSpec as P

AXES = ("expert", "tensor")
OFF = (0, 1, 3, 2)
Z_OFF = (OFF, (0, 3, 1, 2), OFF)
LAST = (2, 0, 1)
MIDDLE = (1, 2, 2)
MASKS = ((1, 3), (3, 1), (1, 3))
ROWS = (48, 48, 32)
VMEM_EXPERTS = 46 * 2**20
FIRST = (0, 48, 96)
BF16 = jnp.bfloat16
F32 = jnp.float32


def device_number(x, y, z, core):
    return (x * 4 + (z % 2) * 2 + core) * 8 + y * 2 + z // 2


def places():
    return [(x, y, z, c) for x in range(4) for y in range(4) for z in range(4) for c in range(2)]


def swap(value, dim, mask):
    pairs = []
    for place in places():
        other = list(place)
        other[dim] ^= mask
        pairs.append((device_number(*place), device_number(*other)))
    return lax.ppermute(value, AXES, pairs)


def from_other_core(value):
    pairs = [(device_number(x, y, z, c), device_number(x, y, z, 1 - c)) for x, y, z, c in places()]
    return lax.ppermute(value, AXES, pairs)


def join(*arrays):
    return jnp.concatenate(arrays, 0)


def gather_last(parts):
    a, b, c = parts
    one_c = swap(c, LAST[2], 1)
    one_a, one_b = swap(a, LAST[0], 1), swap(b, LAST[1], 1)
    three_a, three_b = swap(a, LAST[0], 3), swap(b, LAST[1], 3)
    two_c = swap(one_c, LAST[2], 3)
    c, one_a = lax.optimization_barrier((c, one_a))
    three_c = swap(c, LAST[2], 3)
    two_a = swap(one_a[:8], LAST[0], 3), swap(three_a[8:], LAST[0], 1)
    two_b = swap(one_b[:8], LAST[1], 3), swap(three_b[8:], LAST[1], 1)
    return [a, one_a, three_a, *two_a, b, one_b, three_b, *two_b, c, one_c, three_c, two_c]


def total(own, *others):
    out = own.astype(F32)
    for other in others:
        out = out + other.astype(F32)
    return out.astype(BF16)


def scatter_sums(first, second):
    z_f, x_f, (y_three, y_two) = first[0:4], first[4:8], first[8:]
    z_s, x_s, (y_own, y_one) = second[0:4], second[4:8], second[8:]
    z, x, y = 2, 0, 1
    z_a, x_a = swap(z_f[3], z, 3), swap(x_f[3], x, 3)
    y_a = swap(y_two, y, 3)
    z_b, x_b = swap(z_s[3], z, 1), swap(x_s[3], x, 1)
    y_three = swap(y_three, y, 3)
    y_one = swap(y_one + y_a, y, 1)
    z_one = swap(join(z_f[1] + z_a, z_s[1]), z, 1)
    x_one = swap(join(x_f[1] + x_a, x_s[1]), x, 1)
    z_three = swap(join(z_f[2], z_s[2] + z_b), z, 3)
    x_three = swap(join(x_f[2], x_s[2] + x_b), x, 3)
    x_t = [
        total(x_s[0], x_one[4:], x_three[4:]),
        total(x_f[0], x_one[:4], x_three[:4]),
    ]
    x_t = jnp.concatenate(x_t, 1)
    y_t = total(y_own, y_one, y_three)
    keep = [total(z_s[0], z_one[2:], z_three[2:]), x_t[:2], y_t[:2]]
    send = [total(z_f[0], z_one[:2], z_three[:2]), x_t[2:], y_t[2:]]
    held = [keep[i] + swap(send[i], MIDDLE[i], MASKS[i][1]) for i in range(3)]
    held = [held[i][0] + swap(held[i][1], MIDDLE[i], MASKS[i][0]) for i in range(3)]
    pair = [jnp.concatenate([held[0], held[2]], 1), held[1]]
    for mask, half in ((3, 2), (1, 1)):
        got = [swap(p[half:], dim, mask) for dim, p in enumerate(pair)]
        pair = [p[:half] + g for p, g in zip(pair, got)]
    return join(pair[0][0, :48], pair[1][0], pair[0][0, 48:])


def gathered(refs, i, k3, k2, k1):
    k1 = slice(None) if k1 is None else k1
    group = refs[i * 5 : i * 5 + 5]
    if k3 < 3 or i == 2:
        return group[k3].at[k2, k1]
    return group[3 + k2 // 2].at[k2 % 2, k1]


def spread_out(kys):
    def find(refs, i, k3, k2, k1):
        if i == 0:
            return refs[k3].at[kys.index(k2)]
        if i == 1:
            return refs[4 + k3].at[k2, kys.index(k1)]
        return refs[8 + kys.index(k3)].at[k2]

    return find


def block_pieces(refs, piece, tile, column, ky, bits):
    low, high = bits
    rows = [pl.ds(first, count) for first, count in zip(FIRST, ROWS)]
    kz = [off.index(high * 2 + low) for off in Z_OFF]
    cols = column(ky, high)
    found = [(piece(refs, 0, kz[0], ky, None), tile.at[:, low, rows[0], cols])]
    for kx in range(4):
        found.append((piece(refs, 1, kx, kz[1], ky), tile.at[kx, low, rows[1], cols]))
    found.append((piece(refs, 2, ky, kz[2], None), tile.at[:, low, rows[2], cols]))
    return found


BITS = [(low, high) for low in range(2) for high in range(2)]


def route(ids_ref, mine_ref, gate_col, pick, put):
    before = lax.broadcasted_iota(jnp.int32, (128, 128), 0)
    before = (before < lax.broadcasted_iota(jnp.int32, (128, 128), 1)).astype(BF16)
    number = lax.broadcasted_iota(jnp.int32, (8, 32, 128), 1).astype(F32)
    line = lax.broadcasted_iota(jnp.int32, (8, 128), 0)

    def block(b, carry):
        mine = mine_ref[b].astype(F32)[0:8]
        routes = mine[:, 0:128]
        gates = mine[:, 128:256] + mine[:, 256:384] + mine[:, 384:512]
        named = jnp.zeros((8, 128), F32)
        weight = jnp.zeros((8, 128), F32)
        for e in range(8):
            hit = routes == ids_ref[e]
            any_hit = jnp.max(jnp.where(hit, 1.0, 0.0), axis=0, keepdims=True)
            gate = jnp.sum(jnp.where(hit, gates, 0.0), axis=0, keepdims=True)
            named = jnp.where(line == e, any_hit, named)
            weight = jnp.where(line == e, gate, weight)
        slot = jnp.dot(named.astype(BF16), before, preferred_element_type=F32)
        slot = jnp.where(named > 0, slot, -1.0)
        chosen = slot[:, None, :] == number
        one_hot = jnp.where(chosen, 1.0, 0.0).reshape(256, 128)
        pick[b] = one_hot.astype(BF16)
        put[b] = one_hot.T.astype(BF16)
        rows = pl.ds(pl.multiple_of(b * 32, 32), 32)
        gate_col[:, rows, :] = jnp.sum(
            jnp.where(chosen, weight[:, None, :], 0.0), axis=2, keepdims=True
        )
        return carry

    lax.fori_loop(0, 8, block, 0)


def y_pairs(outs, kys, n, cols_ref, tile):
    def column(ky, high):
        side = lax.rem(cols_ref[ky * 2 + high], 2)
        return pl.ds(pl.multiple_of(side * 512, 512), 512)

    find = spread_out(kys)
    return [
        pair for bits in BITS for pair in block_pieces(outs, find, tile, column, kys[n], bits)
    ]


def columns_of(cols_ref, ky):
    return pl.ds(pl.multiple_of(cols_ref[ky * 2] // 2 * 1024, 1024), 1024)


def expert_kernel(kys, ids_ref, cols_ref, mine_ref, wg, wu, wg2, wu2, wd, wd2, *rest):
    token_refs, rest = rest[:14], rest[14:]
    (h_ref, put), outs = rest[:2], rest[2:-7]
    tokens, sorted_rows, wbuf, gate_col, pick, t_sem, w_sem = rest[-7:]
    d_sem = t_sem.at[0]

    def fetch(e, j, gate, up):
        return [
            pltpu.make_async_copy(gate.at[e], wbuf.at[j, pl.ds(0, 192)], w_sem.at[j, 0]),
            pltpu.make_async_copy(up.at[e], wbuf.at[j, pl.ds(192, 192)], w_sem.at[j, 1]),
        ]

    def load(ky):
        def column(ky, high):
            return pl.ds(pl.multiple_of(cols_ref[ky * 2 + high] * 512, 512), 512)

        pairs = [
            pair
            for bits in BITS
            for pair in block_pieces(token_refs, gathered, tokens, column, ky, bits)
        ]
        return [pltpu.make_async_copy(a, b, t_sem.at[ky, m]) for m, (a, b) in enumerate(pairs)]

    def down_tile(slot, e):
        return wbuf.at[slot, pl.ds(e // 4 * 192, 192), pl.ds(e % 4 * 1024, 1024)]

    def fetch_down(n):
        col = columns_of(cols_ref, kys[n])
        return [
            pltpu.make_async_copy(
                (wd if e < 4 else wd2).at[e % 4, :, col], down_tile(n, e), d_sem.at[n * 8 + e]
            )
            for e in range(8)
        ]

    loads = [load(ky) for ky in range(4)]
    for ky in range(4):
        for copy in loads[ky]:
            copy.start()
    for j in range(2):
        for copy in fetch(j, j, wg, wu):
            copy.start()
    route(ids_ref, mine_ref, gate_col, pick, put)
    for ky in range(4):
        for copy in loads[ky]:
            copy.wait()
        if ky < 2:
            for copy in fetch(ky + 2, ky + 2, wg, wu):
                copy.start()
        col = columns_of(cols_ref, ky)

        def dispatch(b, carry):
            rows = jnp.dot(
                pick[b], tokens[b // 2, lax.rem(b, 2), :, col], preferred_element_type=F32
            )
            rows = rows.astype(BF16).reshape(4, 2, 32, 1024)
            sorted_rows[:, :, pl.ds(pl.multiple_of(b * 32, 32), 32), col] = rows
            return carry

        lax.fori_loop(0, 8, dispatch, 0, unroll=2)

    def experts(turn, carry):
        for j in range(4):
            e = turn * 4 + j
            for copy in fetch(j, j, wg, wu):
                copy.wait()
            act = lax.dot_general(
                sorted_rows[turn * 2 + j // 2, j % 2],
                wbuf[j],
                (((1,), (1,)), ((), ())),
                preferred_element_type=F32,
            )
            gate, up = act[:, :192], act[:, 192:]
            hidden = gate / (1.0 + jnp.exp(-gate)) * up * gate_col[e]
            h_ref[e] = hidden.astype(BF16)

            @pl.when(turn == 0)
            def _():
                for copy in fetch(j, j, wg2, wu2):
                    copy.start()

            if j < 2:

                @pl.when(turn == 1)
                def _():
                    for copy in fetch_down(j):
                        copy.start()

        return carry

    lax.fori_loop(0, 2, experts, 0)
    for n in range(2):
        for copy in fetch_down(n):
            copy.wait()
        for e in range(8):
            out = jnp.dot(h_ref[e], down_tile(n, e)[...], preferred_element_type=F32)
            sorted_rows[:, :, pl.ds(e * 32, 32), pl.ds(0, 1024)] = out.astype(BF16).reshape(
                4, 2, 32, 1024
            )
        col = pl.ds(1024 * (n + 1), 1024)

        def combine(b, carry):
            at = b // 2, lax.rem(b, 2)
            out = jnp.dot(
                put[b], sorted_rows[at[0], at[1], :, pl.ds(0, 1024)], preferred_element_type=F32
            )
            sorted_rows[at[0], at[1], pl.ds(0, 128), col] = out.astype(BF16)
            return carry

        lax.fori_loop(0, 8, combine, 0, unroll=2)
        tile = sorted_rows.at[:, :, pl.ds(0, 128), col]
        stores = [
            pltpu.make_async_copy(b, a, t_sem.at[2 + n, m])
            for m, (a, b) in enumerate(y_pairs(outs, kys, n, cols_ref, tile))
        ]
        for copy in stores:
            copy.start()
        if n == 0:
            first_stores = stores
    for copy in first_stores + stores:
        copy.wait()


def down_kernel(kys, cols_ref, h_ref, put_ref, wd, wd2, *rest):
    outs = rest[:-7]
    h, put, wbuf, expert_rows, ybuf, w_sem, y_sem = rest[-7:]

    def fetch(n):
        col = columns_of(cols_ref, kys[n])
        return [
            pltpu.make_async_copy(wd.at[:, :, col], wbuf.at[n, pl.ds(0, 4)], w_sem.at[n, 0]),
            pltpu.make_async_copy(wd2.at[:, :, col], wbuf.at[n, pl.ds(4, 4)], w_sem.at[n, 1]),
        ]

    def stores(n):
        pairs = y_pairs(outs, kys, n, cols_ref, ybuf.at[n])
        return [pltpu.make_async_copy(b, a, y_sem.at[n, m]) for m, (a, b) in enumerate(pairs)]

    inputs = [
        pltpu.make_async_copy(h_ref, h, w_sem.at[2, 0]),
        pltpu.make_async_copy(put_ref, put, w_sem.at[2, 1]),
    ]
    for copy in inputs + fetch(0) + fetch(1):
        copy.start()
    for copy in inputs:
        copy.wait()
    for n in range(2):
        for copy in fetch(n):
            copy.wait()

        def project(e, carry):
            out = jnp.dot(h[e], wbuf[n, e], preferred_element_type=F32)
            rows = pl.ds(pl.multiple_of(e * 32, 32), 32)
            expert_rows[:, rows] = out.astype(BF16).reshape(8, 32, 1024)
            return carry

        lax.fori_loop(0, 8, project, 0, unroll=2)

        def combine(b, carry):
            out = jnp.dot(put[b], expert_rows[b], preferred_element_type=F32)
            ybuf[n, b // 2, lax.rem(b, 2)] = out.astype(BF16)
            return carry

        lax.fori_loop(0, 8, combine, 0, unroll=2)
        for copy in stores(n):
            copy.start()
    for n in range(2):
        for copy in stores(n):
            copy.wait()


def local(tokens, routes, gates, w_gate, w_up, w_down):
    e, t = lax.axis_index("expert"), lax.axis_index("tensor")
    y, zhi = t // 2, t % 2
    ids = jnp.concatenate([e * 4 + jnp.arange(4), (e ^ 1) * 4 + jnp.arange(4)]).astype(F32)
    cols = jnp.stack([(y ^ OFF[ky]) * 2 + (zhi ^ high) for ky in range(4) for high in range(2)])
    cols = cols.astype(jnp.int32)

    top = lax.reduce_precision(gates, 8, 7)
    rest = gates - top
    middle = lax.reduce_precision(rest, 8, 7)
    packed = jnp.concatenate([part.T for part in (routes.astype(F32), top, middle, rest - middle)], 1)
    packed = jnp.pad(packed.astype(BF16), ((0, 8), (0, 0)))

    wg2 = from_other_core(w_gate)
    along_x = join(tokens[:48], tokens[96:], packed)[None]
    along_y = tokens[48:96][None]
    for mask in (1, 3):
        got = swap(along_x, 0, mask), swap(along_y, 1, mask)
        along_x, along_y = join(along_x, got[0]), join(along_y, got[1])
    along_x, along_y, wg2, w_up = lax.optimization_barrier((along_x, along_y, wg2, w_up))
    wu2 = from_other_core(w_up)
    parts = [along_x[:, :48], along_y, along_x[:, 48:]]
    parts = [join(p, swap(p, MIDDLE[i], MASKS[i][0])) for i, p in enumerate(parts)]
    mine = parts[2][:, 32:].reshape(2, 4, 16, 512)
    mine = jnp.swapaxes(mine, 0, 1).reshape(8, 16, 512)
    parts[2] = parts[2][:, :32]
    parts, wu2, w_down, mine, ids, cols = lax.optimization_barrier(
        (parts, wu2, w_down, mine, ids, cols)
    )
    wd2 = from_other_core(w_down)
    parts = [join(p, swap(p, MIDDLE[i], MASKS[i][1])) for i, p in enumerate(parts)]
    parts, wd2 = lax.optimization_barrier((parts, wd2))
    parts = gather_last(parts)
    pieces = [p.reshape(p.shape[0] // 4, 4, p.shape[1], 512) for p in parts]
    smem = pl.BlockSpec(memory_space=pltpu.SMEM)
    vmem = pl.BlockSpec(memory_space=pltpu.VMEM)
    hbm = pl.BlockSpec(memory_space=pl.ANY)
    shapes = [(2, 4, ROWS[0], 512)] * 4 + [(4, 2, ROWS[1], 512)] * 4
    shapes = [
        jax.ShapeDtypeStruct(shape, BF16) for shape in shapes + [(4, 4, ROWS[2], 512)] * 2
    ]
    hidden, put, *first = pl.pallas_call(
        functools.partial(expert_kernel, (2, 3)),
        out_shape=[
            jax.ShapeDtypeStruct((8, 256, 192), BF16),
            jax.ShapeDtypeStruct((8, 128, 256), BF16),
        ]
        + shapes,
        in_specs=[smem, smem, vmem] + [hbm] * 20,
        out_specs=[vmem, vmem] + [hbm] * 10,
        scratch_shapes=[
            pltpu.VMEM((4, 2, 128, 4096), BF16),
            pltpu.VMEM((4, 2, 256, 4096), BF16),
            pltpu.VMEM((4, 384, 4096), BF16),
            pltpu.VMEM((8, 256, 1), F32),
            pltpu.VMEM((8, 256, 128), BF16),
            pltpu.SemaphoreType.DMA((4, 24)),
            pltpu.SemaphoreType.DMA((4, 2)),
        ],
        compiler_params=pltpu.CompilerParams(vmem_limit_bytes=VMEM_EXPERTS),
        cost_estimate=pl.CostEstimate(
            flops=20 * 10**9, bytes_accessed=50 * 10**6, transcendentals=0
        ),
        name="experts",
    )(ids, cols, mine, w_gate, w_up, wg2, wu2, w_down, wd2, *pieces)

    second = pl.pallas_call(
        functools.partial(down_kernel, (0, 1)),
        out_shape=shapes,
        in_specs=[smem] + [hbm] * 4,
        out_specs=[hbm] * 10,
        scratch_shapes=[
            pltpu.VMEM((8, 256, 192), BF16),
            pltpu.VMEM((8, 128, 256), BF16),
            pltpu.VMEM((2, 8, 192, 1024), BF16),
            pltpu.VMEM((8, 256, 1024), BF16),
            pltpu.VMEM((2, 4, 2, 128, 1024), BF16),
            pltpu.SemaphoreType.DMA((3, 2)),
            pltpu.SemaphoreType.DMA((2, 24)),
        ],
        compiler_params=pltpu.CompilerParams(vmem_limit_bytes=50 * 2**20),
        cost_estimate=pl.CostEstimate(
            flops=6 * 10**9, bytes_accessed=12 * 10**6, transcendentals=0
        ),
        name="down",
    )(cols, hidden, put, w_down, wd2)
    return scatter_sums(first, second)


def solution(mesh):
    placed = (
        P("expert", "tensor"),
        P("expert", None),
        P("expert", None),
        P("expert", "tensor", None),
        P("expert", "tensor", None),
        P("expert", "tensor", None),
    )
    return jax.shard_map(
        local, mesh=mesh, in_specs=placed, out_specs=P("expert", "tensor"), check_vma=False
    )
```

```python
import functools

import jax
import jax.numpy as jnp
from jax import lax
from jax.experimental import pallas as pl
from jax.experimental.pallas import tpu as pltpu
from jax.sharding import PartitionSpec as P

AXES = ("expert", "tensor")
OFF = (0, 1, 3, 2)
Z_OFF = (OFF, (0, 3, 1, 2), OFF)
LAST = (2, 0, 1)
MIDDLE = (1, 2, 2)
MASKS = ((1, 3), (3, 1), (1, 3))
ROWS = (48, 48, 32)
VMEM_EXPERTS = 36 * 2**20
FIRST = (0, 48, 96)
BF16 = jnp.bfloat16
F32 = jnp.float32


def device_number(x, y, z, core):
    return (x * 4 + (z % 2) * 2 + core) * 8 + y * 2 + z // 2


def places():
    return [(x, y, z, c) for x in range(4) for y in range(4) for z in range(4) for c in range(2)]


def swap(value, dim, mask):
    pairs = []
    for place in places():
        other = list(place)
        other[dim] ^= mask
        pairs.append((device_number(*place), device_number(*other)))
    return lax.ppermute(value, AXES, pairs)


def from_other_core(value):
    pairs = [(device_number(x, y, z, c), device_number(x, y, z, 1 - c)) for x, y, z, c in places()]
    return lax.ppermute(value, AXES, pairs)


def join(*arrays):
    return jnp.concatenate(arrays, 0)


def gather_last(parts):
    a, b, c = parts
    one_c = swap(c, LAST[2], 1)
    one_a, one_b = swap(a, LAST[0], 1), swap(b, LAST[1], 1)
    three_a, three_b = swap(a, LAST[0], 3), swap(b, LAST[1], 3)
    two_c = swap(one_c, LAST[2], 3)
    c, one_a = lax.optimization_barrier((c, one_a))
    three_c = swap(c, LAST[2], 3)
    two_a = swap(one_a[:8], LAST[0], 3), swap(three_a[8:], LAST[0], 1)
    two_b = swap(one_b[:8], LAST[1], 3), swap(three_b[8:], LAST[1], 1)
    return [a, one_a, three_a, *two_a, b, one_b, three_b, *two_b, c, one_c, three_c, two_c]


def total(own, *others):
    out = own.astype(F32)
    for other in others:
        out = out + other.astype(F32)
    return out.astype(BF16)


def scatter_sums(first, second):
    z_f, x_f, (y_three, y_two) = first[0:4], first[4:8], first[8:]
    z_s, x_s, (y_own, y_one) = second[0:4], second[4:8], second[8:]
    z, x, y = 2, 0, 1
    z_a, x_a = swap(z_f[3], z, 3), swap(x_f[3], x, 3)
    y_a = swap(y_two, y, 3)
    z_b, x_b = swap(z_s[3], z, 1), swap(x_s[3], x, 1)
    y_three = swap(y_three, y, 3)
    y_one = swap(y_one + y_a, y, 1)
    z_one = swap(join(z_f[1] + z_a, z_s[1]), z, 1)
    x_one = swap(join(x_f[1] + x_a, x_s[1]), x, 1)
    z_three = swap(join(z_f[2], z_s[2] + z_b), z, 3)
    x_three = swap(join(x_f[2], x_s[2] + x_b), x, 3)
    x_t = [
        total(x_s[0], x_one[4:], x_three[4:]),
        total(x_f[0], x_one[:4], x_three[:4]),
    ]
    x_t = jnp.concatenate(x_t, 1)
    y_t = total(y_own, y_one, y_three)
    keep = [total(z_s[0], z_one[2:], z_three[2:]), x_t[:2], y_t[:2]]
    send = [total(z_f[0], z_one[:2], z_three[:2]), x_t[2:], y_t[2:]]
    held = [keep[i] + swap(send[i], MIDDLE[i], MASKS[i][1]) for i in range(3)]
    held = [held[i][0] + swap(held[i][1], MIDDLE[i], MASKS[i][0]) for i in range(3)]
    pair = [jnp.concatenate([held[0], held[2]], 1), held[1]]
    for mask, half in ((3, 2), (1, 1)):
        got = [swap(p[half:], dim, mask) for dim, p in enumerate(pair)]
        pair = [p[:half] + g for p, g in zip(pair, got)]
    return join(pair[0][0, :48], pair[1][0], pair[0][0, 48:])


def gathered(refs, i, k3, k2, k1):
    k1 = slice(None) if k1 is None else k1
    group = refs[i * 5 : i * 5 + 5]
    if k3 < 3 or i == 2:
        return group[k3].at[k2, k1]
    return group[3 + k2 // 2].at[k2 % 2, k1]


def spread_out(kys):
    def find(refs, i, k3, k2, k1):
        if i == 0:
            return refs[k3].at[kys.index(k2)]
        if i == 1:
            return refs[4 + k3].at[k2, kys.index(k1)]
        return refs[8 + kys.index(k3)].at[k2]

    return find


def block_pieces(refs, piece, tile, column, ky, bits):
    low, high = bits
    rows = [pl.ds(first, count) for first, count in zip(FIRST, ROWS)]
    kz = [off.index(high * 2 + low) for off in Z_OFF]
    cols = column(ky, high)
    found = [(piece(refs, 0, kz[0], ky, None), tile.at[:, low, rows[0], cols])]
    for kx in range(4):
        found.append((piece(refs, 1, kx, kz[1], ky), tile.at[kx, low, rows[1], cols]))
    found.append((piece(refs, 2, ky, kz[2], None), tile.at[:, low, rows[2], cols]))
    return found


BITS = [(low, high) for low in range(2) for high in range(2)]


def route(ids_ref, mine_ref, gate_col, pick, put):
    before = lax.broadcasted_iota(jnp.int32, (128, 128), 0)
    before = (before < lax.broadcasted_iota(jnp.int32, (128, 128), 1)).astype(BF16)
    number = lax.broadcasted_iota(jnp.int32, (8, 32, 128), 1).astype(F32)
    line = lax.broadcasted_iota(jnp.int32, (8, 128), 0)

    def block(b, carry):
        mine = mine_ref[b].astype(F32)[0:8]
        routes = mine[:, 0:128]
        gates = mine[:, 128:256] + mine[:, 256:384] + mine[:, 384:512]
        named = jnp.zeros((8, 128), F32)
        weight = jnp.zeros((8, 128), F32)
        for e in range(8):
            hit = routes == ids_ref[e]
            any_hit = jnp.max(jnp.where(hit, 1.0, 0.0), axis=0, keepdims=True)
            gate = jnp.sum(jnp.where(hit, gates, 0.0), axis=0, keepdims=True)
            named = jnp.where(line == e, any_hit, named)
            weight = jnp.where(line == e, gate, weight)
        slot = jnp.dot(named.astype(BF16), before, preferred_element_type=F32)
        slot = jnp.where(named > 0, slot, -1.0)
        chosen = slot[:, None, :] == number
        one_hot = jnp.where(chosen, 1.0, 0.0).reshape(256, 128)
        pick[b] = one_hot.astype(BF16)
        put[b] = one_hot.T.astype(BF16)
        rows = pl.ds(pl.multiple_of(b * 32, 32), 32)
        gate_col[:, rows, :] = jnp.sum(
            jnp.where(chosen, weight[:, None, :], 0.0), axis=2, keepdims=True
        )
        return carry

    lax.fori_loop(0, 8, block, 0)


def y_pairs(outs, kys, n, cols_ref, tile):
    def column(ky, high):
        side = lax.rem(cols_ref[ky * 2 + high], 2)
        return pl.ds(pl.multiple_of(side * 512, 512), 512)

    find = spread_out(kys)
    return [
        pair for bits in BITS for pair in block_pieces(outs, find, tile, column, kys[n], bits)
    ]


def columns_of(cols_ref, ky):
    return pl.ds(pl.multiple_of(cols_ref[ky * 2] // 2 * 1024, 1024), 1024)


def expert_kernel(kys, ids_ref, cols_ref, mine_ref, wg, wu, wg2, wu2, wd, wd2, *rest):
    token_refs, rest = rest[:14], rest[14:]
    (h_ref, put), outs = rest[:2], rest[2:-8]
    tokens, sorted_rows, wbuf, act, gate_col, pick, t_sem, w_sem = rest[-8:]

    def load(ky):
        def column(ky, high):
            return pl.ds(pl.multiple_of(cols_ref[ky * 2 + high] * 512, 512), 512)

        pairs = [
            pair
            for bits in BITS
            for pair in block_pieces(token_refs, gathered, tokens, column, ky, bits)
        ]
        return [pltpu.make_async_copy(a, b, t_sem.at[ky, m]) for m, (a, b) in enumerate(pairs)]

    def fetch(ky):
        col, slot = columns_of(cols_ref, ky), ky % 2
        places = [(w, first, row) for first, pair in ((0, (wg, wu)), (4, (wg2, wu2)))
                  for row, w in zip((0, 192), pair)]
        return [
            pltpu.make_async_copy(
                w.at[:, :, col], wbuf.at[slot, pl.ds(first, 4), pl.ds(row, 192)], w_sem.at[slot, m]
            )
            for m, (w, first, row) in enumerate(places)
        ]

    def fetch_down(n):
        col = columns_of(cols_ref, kys[n])
        return [
            pltpu.make_async_copy(
                w.at[:, :, col],
                wbuf.at[0, pl.ds(first, 4), pl.ds(n * 192, 192)],
                w_sem.at[0, n * 2 + m],
            )
            for m, (w, first) in enumerate(((wd, 0), (wd2, 4)))
        ]

    def start(copies):
        for copy in copies:
            copy.start()

    def finish(copies):
        for copy in copies:
            copy.wait()

    for ky in range(2):
        start(load(ky))
        start(fetch(ky))
    route(ids_ref, mine_ref, gate_col, pick, put)
    for ky in range(4):
        finish(load(ky))
        if ky < 2:
            start(load(ky + 2))
        col = columns_of(cols_ref, ky)

        def dispatch(b, carry):
            rows = jnp.dot(
                pick[b], tokens[b // 2, lax.rem(b, 2), :, col], preferred_element_type=F32
            )
            rows = rows.astype(BF16).reshape(4, 2, 32, 1024)
            sorted_rows[:, :, pl.ds(pl.multiple_of(b * 32, 32), 32)] = rows
            return carry

        lax.fori_loop(0, 8, dispatch, 0, unroll=4)
        finish(fetch(ky))

        def project(e, carry):
            part = lax.dot_general(
                sorted_rows[e // 2, lax.rem(e, 2)],
                wbuf[ky % 2, e],
                (((1,), (1,)), ((), ())),
                preferred_element_type=F32,
            )
            if ky > 0:
                part = act[e] + part
            if ky < 3:
                act[e] = part
            else:
                gate, up = part[:, :192], part[:, 192:]
                h_ref[e] = (gate / (1.0 + jnp.exp(-gate)) * up * gate_col[e]).astype(BF16)
            return carry

        lax.fori_loop(0, 8, project, 0, unroll=4)
        if ky < 2:
            start(fetch(ky + 2))
        if ky == 2:
            start(fetch_down(0) + fetch_down(1))
    stores = []
    for n in range(2):
        finish(fetch_down(n))

        def project_out(e, carry):
            down = wbuf[0, e, pl.ds(n * 192, 192)]
            out = jnp.dot(h_ref[e], down, preferred_element_type=F32)
            rows = pl.ds(pl.multiple_of(e * 32, 32), 32)
            sorted_rows[:, :, rows] = out.astype(BF16).reshape(4, 2, 32, 1024)
            return carry

        lax.fori_loop(0, 8, project_out, 0, unroll=4)
        col = pl.ds(1024 * n, 1024)

        def combine(b, carry):
            at = b // 2, lax.rem(b, 2)
            out = jnp.dot(put[b], sorted_rows[at[0], at[1]], preferred_element_type=F32)
            tokens[at[0], at[1], :, col] = out.astype(BF16)
            return carry

        lax.fori_loop(0, 8, combine, 0, unroll=4)
        pairs = y_pairs(outs, kys, n, cols_ref, tokens.at[:, :, :, col])
        stores.append(
            [pltpu.make_async_copy(b, a, t_sem.at[n, m]) for m, (a, b) in enumerate(pairs)]
        )
        start(stores[n])
    finish(stores[0] + stores[1])


def down_kernel(kys, cols_ref, h_ref, put_ref, wd, wd2, *rest):
    outs = rest[:-7]
    h, put, wbuf, expert_rows, ybuf, w_sem, y_sem = rest[-7:]

    def fetch(n):
        col = columns_of(cols_ref, kys[n])
        return [
            pltpu.make_async_copy(wd.at[:, :, col], wbuf.at[n, pl.ds(0, 4)], w_sem.at[n, 0]),
            pltpu.make_async_copy(wd2.at[:, :, col], wbuf.at[n, pl.ds(4, 4)], w_sem.at[n, 1]),
        ]

    def stores(n):
        pairs = y_pairs(outs, kys, n, cols_ref, ybuf.at[n])
        return [pltpu.make_async_copy(b, a, y_sem.at[n, m]) for m, (a, b) in enumerate(pairs)]

    inputs = [
        pltpu.make_async_copy(h_ref, h, w_sem.at[2, 0]),
        pltpu.make_async_copy(put_ref, put, w_sem.at[2, 1]),
    ]
    for copy in inputs + fetch(0) + fetch(1):
        copy.start()
    for copy in inputs:
        copy.wait()
    for n in range(2):
        for copy in fetch(n):
            copy.wait()

        def project(e, carry):
            out = jnp.dot(h[e], wbuf[n, e], preferred_element_type=F32)
            rows = pl.ds(pl.multiple_of(e * 32, 32), 32)
            expert_rows[:, rows] = out.astype(BF16).reshape(8, 32, 1024)
            return carry

        lax.fori_loop(0, 8, project, 0, unroll=4)

        def combine(b, carry):
            out = jnp.dot(put[b], expert_rows[b], preferred_element_type=F32)
            ybuf[n, b // 2, lax.rem(b, 2)] = out.astype(BF16)
            return carry

        lax.fori_loop(0, 8, combine, 0, unroll=4)
        for copy in stores(n):
            copy.start()
    for n in range(2):
        for copy in stores(n):
            copy.wait()


def local(tokens, routes, gates, w_gate, w_up, w_down):
    e, t = lax.axis_index("expert"), lax.axis_index("tensor")
    y, zhi = t // 2, t % 2
    ids = jnp.concatenate([e * 4 + jnp.arange(4), (e ^ 1) * 4 + jnp.arange(4)]).astype(F32)
    cols = jnp.stack([(y ^ OFF[ky]) * 2 + (zhi ^ high) for ky in range(4) for high in range(2)])
    cols = cols.astype(jnp.int32)

    top = lax.reduce_precision(gates, 8, 7)
    rest = gates - top
    middle = lax.reduce_precision(rest, 8, 7)
    packed = jnp.concatenate([part.T for part in (routes.astype(F32), top, middle, rest - middle)], 1)
    packed = jnp.pad(packed.astype(BF16), ((0, 8), (0, 0)))

    wg2 = from_other_core(w_gate)
    along_x = join(tokens[:48], tokens[96:], packed)[None]
    along_y = tokens[48:96][None]
    for mask in (1, 3):
        got = swap(along_x, 0, mask), swap(along_y, 1, mask)
        along_x, along_y = join(along_x, got[0]), join(along_y, got[1])
    along_x, along_y, wg2, w_up = lax.optimization_barrier((along_x, along_y, wg2, w_up))
    wu2 = from_other_core(w_up)
    parts = [along_x[:, :48], along_y, along_x[:, 48:]]
    parts = [join(p, swap(p, MIDDLE[i], MASKS[i][0])) for i, p in enumerate(parts)]
    mine = parts[2][:, 32:].reshape(2, 4, 16, 512)
    mine = jnp.swapaxes(mine, 0, 1).reshape(8, 16, 512)
    parts[2] = parts[2][:, :32]
    parts, wu2, w_down, mine, ids, cols = lax.optimization_barrier(
        (parts, wu2, w_down, mine, ids, cols)
    )
    wd2 = from_other_core(w_down)
    parts = [join(p, swap(p, MIDDLE[i], MASKS[i][1])) for i, p in enumerate(parts)]
    parts, wd2 = lax.optimization_barrier((parts, wd2))
    parts = gather_last(parts)
    pieces = [p.reshape(p.shape[0] // 4, 4, p.shape[1], 512) for p in parts]
    smem = pl.BlockSpec(memory_space=pltpu.SMEM)
    vmem = pl.BlockSpec(memory_space=pltpu.VMEM)
    hbm = pl.BlockSpec(memory_space=pl.ANY)
    shapes = [(2, 4, ROWS[0], 512)] * 4 + [(4, 2, ROWS[1], 512)] * 4
    shapes = [
        jax.ShapeDtypeStruct(shape, BF16) for shape in shapes + [(4, 4, ROWS[2], 512)] * 2
    ]
    hidden, put, *first = pl.pallas_call(
        functools.partial(expert_kernel, (2, 3)),
        out_shape=[
            jax.ShapeDtypeStruct((8, 256, 192), BF16),
            jax.ShapeDtypeStruct((8, 128, 256), BF16),
        ]
        + shapes,
        in_specs=[smem, smem, vmem] + [hbm] * 20,
        out_specs=[vmem, vmem] + [hbm] * 10,
        scratch_shapes=[
            pltpu.VMEM((4, 2, 128, 4096), BF16),
            pltpu.VMEM((4, 2, 256, 1024), BF16),
            pltpu.VMEM((2, 8, 384, 1024), BF16),
            pltpu.VMEM((8, 256, 384), F32),
            pltpu.VMEM((8, 256, 1), F32),
            pltpu.VMEM((8, 256, 128), BF16),
            pltpu.SemaphoreType.DMA((4, 24)),
            pltpu.SemaphoreType.DMA((2, 4)),
        ],
        compiler_params=pltpu.CompilerParams(vmem_limit_bytes=VMEM_EXPERTS),
        cost_estimate=pl.CostEstimate(
            flops=20 * 10**9, bytes_accessed=50 * 10**6, transcendentals=0
        ),
        name="experts",
    )(ids, cols, mine, w_gate, w_up, wg2, wu2, w_down, wd2, *pieces)

    second = pl.pallas_call(
        functools.partial(down_kernel, (0, 1)),
        out_shape=shapes,
        in_specs=[smem] + [hbm] * 4,
        out_specs=[hbm] * 10,
        scratch_shapes=[
            pltpu.VMEM((8, 256, 192), BF16),
            pltpu.VMEM((8, 128, 256), BF16),
            pltpu.VMEM((2, 8, 192, 1024), BF16),
            pltpu.VMEM((8, 256, 1024), BF16),
            pltpu.VMEM((2, 4, 2, 128, 1024), BF16),
            pltpu.SemaphoreType.DMA((3, 2)),
            pltpu.SemaphoreType.DMA((2, 24)),
        ],
        compiler_params=pltpu.CompilerParams(vmem_limit_bytes=50 * 2**20),
        cost_estimate=pl.CostEstimate(
            flops=6 * 10**9, bytes_accessed=12 * 10**6, transcendentals=0
        ),
        name="down",
    )(cols, hidden, put, w_down, wd2)
    return scatter_sums(first, second)


def solution(mesh):
    placed = (
        P("expert", "tensor"),
        P("expert", None),
        P("expert", None),
        P("expert", "tensor", None),
        P("expert", "tensor", None),
        P("expert", "tensor", None),
    )
    return jax.shard_map(
        local, mesh=mesh, in_specs=placed, out_specs=P("expert", "tensor"), check_vma=False
    )
```

```python
import functools

import jax
import jax.numpy as jnp
from jax import lax
from jax.experimental import pallas as pl
from jax.experimental.pallas import tpu as pltpu
from jax.sharding import PartitionSpec as P

AXES = ("expert", "tensor")
OFF = (0, 1, 3, 2)
Z_OFF = (OFF, (0, 3, 1, 2), OFF)
LAST = (2, 0, 1)
MIDDLE = (1, 2, 2)
MASKS = ((1, 3), (3, 1), (1, 3))
ROWS = (48, 48, 32)
VMEM_EXPERTS = 36 * 2**20
FIRST = (0, 48, 96)
BF16 = jnp.bfloat16
F32 = jnp.float32


def device_number(x, y, z, core):
    return (x * 4 + (z % 2) * 2 + core) * 8 + y * 2 + z // 2


def places():
    return [(x, y, z, c) for x in range(4) for y in range(4) for z in range(4) for c in range(2)]


def swap(value, dim, mask):
    pairs = []
    for place in places():
        other = list(place)
        other[dim] ^= mask
        pairs.append((device_number(*place), device_number(*other)))
    return lax.ppermute(value, AXES, pairs)


def from_other_core(value):
    pairs = [(device_number(x, y, z, c), device_number(x, y, z, 1 - c)) for x, y, z, c in places()]
    return lax.ppermute(value, AXES, pairs)


def join(*arrays):
    return jnp.concatenate(arrays, 0)


def gather_last(parts):
    a, b, c = parts
    one_c = swap(c, LAST[2], 1)
    one_a, one_b = swap(a, LAST[0], 1), swap(b, LAST[1], 1)
    three_a, three_b = swap(a, LAST[0], 3), swap(b, LAST[1], 3)
    two_c = swap(one_c, LAST[2], 3)
    c, one_a = lax.optimization_barrier((c, one_a))
    three_c = swap(c, LAST[2], 3)
    two_a = swap(one_a[:8], LAST[0], 3), swap(three_a[8:], LAST[0], 1)
    two_b = swap(one_b[:8], LAST[1], 3), swap(three_b[8:], LAST[1], 1)
    return [a, one_a, three_a, *two_a, b, one_b, three_b, *two_b, c, one_c, three_c, two_c]


def total(own, *others):
    out = own.astype(F32)
    for other in others:
        out = out + other.astype(F32)
    return out.astype(BF16)


def scatter_sums(first, second):
    z_f, x_f, (y_three, y_two) = first[0:4], first[4:8], first[8:]
    z_s, x_s, (y_own, y_one) = second[0:4], second[4:8], second[8:]
    z, x, y = 2, 0, 1
    z_a, x_a = swap(z_f[3], z, 3), swap(x_f[3], x, 3)
    y_a = swap(y_two, y, 3)
    z_b, x_b = swap(z_s[3], z, 1), swap(x_s[3], x, 1)
    y_three = swap(y_three, y, 3)
    y_one = swap(y_one + y_a, y, 1)
    z_one = swap(join(z_f[1] + z_a, z_s[1]), z, 1)
    x_one = swap(join(x_f[1] + x_a, x_s[1]), x, 1)
    z_three = swap(join(z_f[2], z_s[2] + z_b), z, 3)
    x_three = swap(join(x_f[2], x_s[2] + x_b), x, 3)
    x_t = [
        total(x_s[0], x_one[4:], x_three[4:]),
        total(x_f[0], x_one[:4], x_three[:4]),
    ]
    x_t = jnp.concatenate(x_t, 1)
    y_t = total(y_own, y_one, y_three)
    keep = [total(z_s[0], z_one[2:], z_three[2:]), x_t[:2], y_t[:2]]
    send = [total(z_f[0], z_one[:2], z_three[:2]), x_t[2:], y_t[2:]]
    held = [keep[i] + swap(send[i], MIDDLE[i], MASKS[i][1]) for i in range(3)]
    held = [held[i][0] + swap(held[i][1], MIDDLE[i], MASKS[i][0]) for i in range(3)]
    pair = [jnp.concatenate([held[0], held[2]], 1), held[1]]
    for mask, half in ((3, 2), (1, 1)):
        got = [swap(p[half:], dim, mask) for dim, p in enumerate(pair)]
        pair = [p[:half] + g for p, g in zip(pair, got)]
    return join(pair[0][0, :48], pair[1][0], pair[0][0, 48:])


def gathered(refs, i, k3, k2, k1):
    k1 = slice(None) if k1 is None else k1
    group = refs[i * 5 : i * 5 + 5]
    if k3 < 3 or i == 2:
        return group[k3].at[k2, k1]
    return group[3 + k2 // 2].at[k2 % 2, k1]


def spread_out(kys):
    def find(refs, i, k3, k2, k1):
        if i == 0:
            return refs[k3].at[kys.index(k2)]
        if i == 1:
            return refs[4 + k3].at[k2, kys.index(k1)]
        return refs[8 + kys.index(k3)].at[k2]

    return find


def block_pieces(refs, piece, tile, column, ky, bits):
    low, high = bits
    rows = [pl.ds(first, count) for first, count in zip(FIRST, ROWS)]
    kz = [off.index(high * 2 + low) for off in Z_OFF]
    cols = column(ky, high)
    found = [(piece(refs, 0, kz[0], ky, None), tile.at[:, low, rows[0], cols])]
    for kx in range(4):
        found.append((piece(refs, 1, kx, kz[1], ky), tile.at[kx, low, rows[1], cols]))
    found.append((piece(refs, 2, ky, kz[2], None), tile.at[:, low, rows[2], cols]))
    return found


BITS = [(low, high) for low in range(2) for high in range(2)]


def route(ids_ref, mine_ref, gate_col, pick, put):
    before = lax.broadcasted_iota(jnp.int32, (128, 128), 0)
    before = (before < lax.broadcasted_iota(jnp.int32, (128, 128), 1)).astype(BF16)
    number = lax.broadcasted_iota(jnp.int32, (8, 32, 128), 1).astype(F32)
    line = lax.broadcasted_iota(jnp.int32, (8, 128), 0)

    def block(b, carry):
        mine = mine_ref[b].astype(F32)[0:8]
        routes = mine[:, 0:128]
        gates = mine[:, 128:256] + mine[:, 256:384] + mine[:, 384:512]
        named = jnp.zeros((8, 128), F32)
        weight = jnp.zeros((8, 128), F32)
        for e in range(8):
            hit = routes == ids_ref[e]
            any_hit = jnp.max(jnp.where(hit, 1.0, 0.0), axis=0, keepdims=True)
            gate = jnp.sum(jnp.where(hit, gates, 0.0), axis=0, keepdims=True)
            named = jnp.where(line == e, any_hit, named)
            weight = jnp.where(line == e, gate, weight)
        slot = jnp.dot(named.astype(BF16), before, preferred_element_type=F32)
        slot = jnp.where(named > 0, slot, -1.0)
        chosen = slot[:, None, :] == number
        one_hot = jnp.where(chosen, 1.0, 0.0).reshape(256, 128)
        pick[b] = one_hot.astype(BF16)
        put[b] = one_hot.T.astype(BF16)
        rows = pl.ds(pl.multiple_of(b * 32, 32), 32)
        gate_col[:, rows, :] = jnp.sum(
            jnp.where(chosen, weight[:, None, :], 0.0), axis=2, keepdims=True
        )
        return carry

    lax.fori_loop(0, 8, block, 0)


def y_pairs(outs, kys, n, cols_ref, tile):
    def column(ky, high):
        side = lax.rem(cols_ref[ky * 2 + high], 2)
        return pl.ds(pl.multiple_of(side * 512, 512), 512)

    find = spread_out(kys)
    return [
        pair for bits in BITS for pair in block_pieces(outs, find, tile, column, kys[n], bits)
    ]


def columns_of(cols_ref, ky):
    return pl.ds(pl.multiple_of(cols_ref[ky * 2] // 2 * 1024, 1024), 1024)


def expert_kernel(kys, ids_ref, cols_ref, mine_ref, wg, wu, wg2, wu2, wd, wd2, *rest):
    token_refs, rest = rest[:14], rest[14:]
    (h_ref, put), outs = rest[:2], rest[2:-8]
    tokens, sorted_rows, wbuf, act, gate_col, pick, t_sem, w_sem = rest[-8:]

    def load(ky):
        def column(ky, high):
            return pl.ds(pl.multiple_of(cols_ref[ky * 2 + high] * 512, 512), 512)

        pairs = [
            pair
            for bits in BITS
            for pair in block_pieces(token_refs, gathered, tokens, column, ky, bits)
        ]
        return [pltpu.make_async_copy(a, b, t_sem.at[ky, m]) for m, (a, b) in enumerate(pairs)]

    def fetch(ky):
        col, slot = columns_of(cols_ref, ky), ky % 2
        places = [(w, first, row) for first, pair in ((0, (wg, wu)), (4, (wg2, wu2)))
                  for row, w in zip((0, 192), pair)]
        return [
            pltpu.make_async_copy(
                w.at[:, :, col], wbuf.at[slot, pl.ds(first, 4), pl.ds(row, 192)], w_sem.at[slot, m]
            )
            for m, (w, first, row) in enumerate(places)
        ]

    def fetch_down(n):
        col = columns_of(cols_ref, kys[n])
        return [
            pltpu.make_async_copy(
                w.at[:, :, col],
                wbuf.at[0, pl.ds(first, 4), pl.ds(n * 192, 192)],
                w_sem.at[0, n * 2 + m],
            )
            for m, (w, first) in enumerate(((wd, 0), (wd2, 4)))
        ]

    def start(copies):
        for copy in copies:
            copy.start()

    def finish(copies):
        for copy in copies:
            copy.wait()

    for ky in range(2):
        start(load(ky))
        start(fetch(ky))
    route(ids_ref, mine_ref, gate_col, pick, put)
    for ky in range(4):
        finish(load(ky))
        if ky < 2:
            start(load(ky + 2))
        col = columns_of(cols_ref, ky)

        def dispatch(b, carry):
            rows = jnp.dot(
                pick[b], tokens[b // 2, lax.rem(b, 2), :, col], preferred_element_type=F32
            )
            rows = rows.astype(BF16).reshape(4, 2, 32, 1024)
            sorted_rows[:, :, pl.ds(pl.multiple_of(b * 32, 32), 32)] = rows
            return carry

        lax.fori_loop(0, 8, dispatch, 0, unroll=8)
        finish(fetch(ky))

        def project(e, carry):
            part = lax.dot_general(
                sorted_rows[e // 2, lax.rem(e, 2)],
                wbuf[ky % 2, e],
                (((1,), (1,)), ((), ())),
                preferred_element_type=F32,
            )
            if ky > 0:
                part = act[e] + part
            if ky < 3:
                act[e] = part
            else:
                gate, up = part[:, :192], part[:, 192:]
                h_ref[e] = (gate / (1.0 + jnp.exp(-gate)) * up * gate_col[e]).astype(BF16)
            return carry

        lax.fori_loop(0, 8, project, 0, unroll=8)
        if ky < 2:
            start(fetch(ky + 2))
        if ky == 2:
            start(fetch_down(0) + fetch_down(1))
    stores = []
    for n in range(2):
        finish(fetch_down(n))

        def project_out(e, carry):
            down = wbuf[0, e, pl.ds(n * 192, 192)]
            out = jnp.dot(h_ref[e], down, preferred_element_type=F32)
            rows = pl.ds(pl.multiple_of(e * 32, 32), 32)
            sorted_rows[:, :, rows] = out.astype(BF16).reshape(4, 2, 32, 1024)
            return carry

        lax.fori_loop(0, 8, project_out, 0, unroll=8)
        col = pl.ds(1024 * n, 1024)

        def combine(b, carry):
            at = b // 2, lax.rem(b, 2)
            out = jnp.dot(put[b], sorted_rows[at[0], at[1]], preferred_element_type=F32)
            tokens[at[0], at[1], :, col] = out.astype(BF16)
            return carry

        lax.fori_loop(0, 8, combine, 0, unroll=8)
        pairs = y_pairs(outs, kys, n, cols_ref, tokens.at[:, :, :, col])
        stores.append(
            [pltpu.make_async_copy(b, a, t_sem.at[n, m]) for m, (a, b) in enumerate(pairs)]
        )
        start(stores[n])
    finish(stores[0] + stores[1])


def down_kernel(kys, cols_ref, h_ref, put_ref, wd, wd2, *rest):
    outs = rest[:-7]
    h, put, wbuf, expert_rows, ybuf, w_sem, y_sem = rest[-7:]

    def fetch(n):
        col = columns_of(cols_ref, kys[n])
        return [
            pltpu.make_async_copy(wd.at[:, :, col], wbuf.at[n, pl.ds(0, 4)], w_sem.at[n, 0]),
            pltpu.make_async_copy(wd2.at[:, :, col], wbuf.at[n, pl.ds(4, 4)], w_sem.at[n, 1]),
        ]

    def stores(n):
        pairs = y_pairs(outs, kys, n, cols_ref, ybuf.at[n])
        return [pltpu.make_async_copy(b, a, y_sem.at[n, m]) for m, (a, b) in enumerate(pairs)]

    inputs = [
        pltpu.make_async_copy(h_ref, h, w_sem.at[2, 0]),
        pltpu.make_async_copy(put_ref, put, w_sem.at[2, 1]),
    ]
    for copy in inputs + fetch(0) + fetch(1):
        copy.start()
    for copy in inputs:
        copy.wait()
    for n in range(2):
        for copy in fetch(n):
            copy.wait()

        def project(e, carry):
            out = jnp.dot(h[e], wbuf[n, e], preferred_element_type=F32)
            rows = pl.ds(pl.multiple_of(e * 32, 32), 32)
            expert_rows[:, rows] = out.astype(BF16).reshape(8, 32, 1024)
            return carry

        lax.fori_loop(0, 8, project, 0, unroll=4)

        def combine(b, carry):
            out = jnp.dot(put[b], expert_rows[b], preferred_element_type=F32)
            ybuf[n, b // 2, lax.rem(b, 2)] = out.astype(BF16)
            return carry

        lax.fori_loop(0, 8, combine, 0, unroll=8)
        for copy in stores(n):
            copy.start()
    for n in range(2):
        for copy in stores(n):
            copy.wait()


def local(tokens, routes, gates, w_gate, w_up, w_down):
    e, t = lax.axis_index("expert"), lax.axis_index("tensor")
    y, zhi = t // 2, t % 2
    ids = jnp.concatenate([e * 4 + jnp.arange(4), (e ^ 1) * 4 + jnp.arange(4)]).astype(F32)
    cols = jnp.stack([(y ^ OFF[ky]) * 2 + (zhi ^ high) for ky in range(4) for high in range(2)])
    cols = cols.astype(jnp.int32)

    top = lax.reduce_precision(gates, 8, 7)
    rest = gates - top
    middle = lax.reduce_precision(rest, 8, 7)
    packed = jnp.concatenate([part.T for part in (routes.astype(F32), top, middle, rest - middle)], 1)
    packed = jnp.pad(packed.astype(BF16), ((0, 8), (0, 0)))

    wg2 = from_other_core(w_gate)
    along_x = join(tokens[:48], tokens[96:], packed)[None]
    along_y = tokens[48:96][None]
    for mask in (1, 3):
        got = swap(along_x, 0, mask), swap(along_y, 1, mask)
        along_x, along_y = join(along_x, got[0]), join(along_y, got[1])
    along_x, along_y, wg2, w_up = lax.optimization_barrier((along_x, along_y, wg2, w_up))
    wu2 = from_other_core(w_up)
    parts = [along_x[:, :48], along_y, along_x[:, 48:]]
    parts = [join(p, swap(p, MIDDLE[i], MASKS[i][0])) for i, p in enumerate(parts)]
    mine = parts[2][:, 32:].reshape(2, 4, 16, 512)
    mine = jnp.swapaxes(mine, 0, 1).reshape(8, 16, 512)
    parts[2] = parts[2][:, :32]
    parts, wu2, w_down, mine, ids, cols = lax.optimization_barrier(
        (parts, wu2, w_down, mine, ids, cols)
    )
    wd2 = from_other_core(w_down)
    parts = [join(p, swap(p, MIDDLE[i], MASKS[i][1])) for i, p in enumerate(parts)]
    parts, wd2 = lax.optimization_barrier((parts, wd2))
    parts = gather_last(parts)
    pieces = [p.reshape(p.shape[0] // 4, 4, p.shape[1], 512) for p in parts]
    smem = pl.BlockSpec(memory_space=pltpu.SMEM)
    vmem = pl.BlockSpec(memory_space=pltpu.VMEM)
    hbm = pl.BlockSpec(memory_space=pl.ANY)
    shapes = [(2, 4, ROWS[0], 512)] * 4 + [(4, 2, ROWS[1], 512)] * 4
    shapes = [
        jax.ShapeDtypeStruct(shape, BF16) for shape in shapes + [(4, 4, ROWS[2], 512)] * 2
    ]
    hidden, put, *first = pl.pallas_call(
        functools.partial(expert_kernel, (2, 3)),
        out_shape=[
            jax.ShapeDtypeStruct((8, 256, 192), BF16),
            jax.ShapeDtypeStruct((8, 128, 256), BF16),
        ]
        + shapes,
        in_specs=[smem, smem, vmem] + [hbm] * 20,
        out_specs=[vmem, vmem] + [hbm] * 10,
        scratch_shapes=[
            pltpu.VMEM((4, 2, 128, 4096), BF16),
            pltpu.VMEM((4, 2, 256, 1024), BF16),
            pltpu.VMEM((2, 8, 384, 1024), BF16),
            pltpu.VMEM((8, 256, 384), F32),
            pltpu.VMEM((8, 256, 1), F32),
            pltpu.VMEM((8, 256, 128), BF16),
            pltpu.SemaphoreType.DMA((4, 24)),
            pltpu.SemaphoreType.DMA((2, 4)),
        ],
        compiler_params=pltpu.CompilerParams(vmem_limit_bytes=VMEM_EXPERTS),
        cost_estimate=pl.CostEstimate(
            flops=20 * 10**9, bytes_accessed=50 * 10**6, transcendentals=0
        ),
        name="experts",
    )(ids, cols, mine, w_gate, w_up, wg2, wu2, w_down, wd2, *pieces)

    second = pl.pallas_call(
        functools.partial(down_kernel, (0, 1)),
        out_shape=shapes,
        in_specs=[smem] + [hbm] * 4,
        out_specs=[hbm] * 10,
        scratch_shapes=[
            pltpu.VMEM((8, 256, 192), BF16),
            pltpu.VMEM((8, 128, 256), BF16),
            pltpu.VMEM((2, 8, 192, 1024), BF16),
            pltpu.VMEM((8, 256, 1024), BF16),
            pltpu.VMEM((2, 4, 2, 128, 1024), BF16),
            pltpu.SemaphoreType.DMA((3, 2)),
            pltpu.SemaphoreType.DMA((2, 24)),
        ],
        compiler_params=pltpu.CompilerParams(vmem_limit_bytes=50 * 2**20),
        cost_estimate=pl.CostEstimate(
            flops=6 * 10**9, bytes_accessed=12 * 10**6, transcendentals=0
        ),
        name="down",
    )(cols, hidden, put, w_down, wd2)
    return scatter_sums(first, second)


def solution(mesh):
    placed = (
        P("expert", "tensor"),
        P("expert", None),
        P("expert", None),
        P("expert", "tensor", None),
        P("expert", "tensor", None),
        P("expert", "tensor", None),
    )
    return jax.shard_map(
        local, mesh=mesh, in_specs=placed, out_specs=P("expert", "tensor"), check_vma=False
    )
```

```python
import functools

import jax
import jax.numpy as jnp
from jax import lax
from jax.experimental import pallas as pl
from jax.experimental.pallas import tpu as pltpu
from jax.sharding import PartitionSpec as P

AXES = ("expert", "tensor")
OFF = (0, 1, 3, 2)
Z_OFF = (OFF, (0, 3, 1, 2), OFF)
LAST = (2, 0, 1)
MIDDLE = (1, 2, 2)
MASKS = ((1, 3), (3, 1), (1, 3))
ROWS = (48, 48, 32)
VMEM_EXPERTS = 36 * 2**20
FIRST = (0, 48, 96)
BF16 = jnp.bfloat16
F32 = jnp.float32


def device_number(x, y, z, core):
    return (x * 4 + (z % 2) * 2 + core) * 8 + y * 2 + z // 2


def places():
    return [(x, y, z, c) for x in range(4) for y in range(4) for z in range(4) for c in range(2)]


def swap(value, dim, mask):
    pairs = []
    for place in places():
        other = list(place)
        other[dim] ^= mask
        pairs.append((device_number(*place), device_number(*other)))
    return lax.ppermute(value, AXES, pairs)


def from_other_core(value):
    pairs = [(device_number(x, y, z, c), device_number(x, y, z, 1 - c)) for x, y, z, c in places()]
    return lax.ppermute(value, AXES, pairs)


def join(*arrays):
    return jnp.concatenate(arrays, 0)


def gather_last(parts):
    a, b, c = parts
    one_c = swap(c, LAST[2], 1)
    one_a, one_b = swap(a, LAST[0], 1), swap(b, LAST[1], 1)
    three_a, three_b = swap(a, LAST[0], 3), swap(b, LAST[1], 3)
    c, one_c = lax.optimization_barrier((c, one_c))
    three_c = swap(c, LAST[2], 3)
    two_c = swap(one_c, LAST[2], 3)
    two_a = swap(one_a[:8], LAST[0], 3), swap(three_a[8:], LAST[0], 1)
    two_b = swap(one_b[:8], LAST[1], 3), swap(three_b[8:], LAST[1], 1)
    return [a, one_a, three_a, *two_a, b, one_b, three_b, *two_b, c, one_c, three_c, two_c]


def total(own, *others):
    out = own.astype(F32)
    for other in others:
        out = out + other.astype(F32)
    return out.astype(BF16)


def scatter_sums(first, second):
    z_f, x_f, (y_three, y_two) = first[0:4], first[4:8], first[8:]
    z_s, x_s, (y_own, y_one) = second[0:4], second[4:8], second[8:]
    z, x, y = 2, 0, 1
    z_a, x_a = swap(z_f[3], z, 3), swap(x_f[3], x, 3)
    y_a = swap(y_two, y, 3)
    z_b, x_b = swap(z_s[3], z, 1), swap(x_s[3], x, 1)
    y_three = swap(y_three, y, 3)
    y_one = swap(y_one + y_a, y, 1)
    z_one = swap(join(z_f[1] + z_a, z_s[1]), z, 1)
    x_one = swap(join(x_f[1] + x_a, x_s[1]), x, 1)
    z_three = swap(join(z_f[2], z_s[2] + z_b), z, 3)
    x_three = swap(join(x_f[2], x_s[2] + x_b), x, 3)
    x_t = [
        total(x_s[0], x_one[4:], x_three[4:]),
        total(x_f[0], x_one[:4], x_three[:4]),
    ]
    x_t = jnp.concatenate(x_t, 1)
    y_t = total(y_own, y_one, y_three)
    keep = [total(z_s[0], z_one[2:], z_three[2:]), x_t[:2], y_t[:2]]
    send = [total(z_f[0], z_one[:2], z_three[:2]), x_t[2:], y_t[2:]]
    held = [keep[i] + swap(send[i], MIDDLE[i], MASKS[i][1]) for i in range(3)]
    held = [held[i][0] + swap(held[i][1], MIDDLE[i], MASKS[i][0]) for i in range(3)]
    pair = [jnp.concatenate([held[0], held[2]], 1), held[1]]
    for mask, half in ((3, 2), (1, 1)):
        got = [swap(p[half:], dim, mask) for dim, p in enumerate(pair)]
        pair = [p[:half] + g for p, g in zip(pair, got)]
    return join(pair[0][0, :48], pair[1][0], pair[0][0, 48:])


def gathered(refs, i, k3, k2, k1):
    k1 = slice(None) if k1 is None else k1
    group = refs[i * 5 : i * 5 + 5]
    if k3 < 3 or i == 2:
        return group[k3].at[k2, k1]
    return group[3 + k2 // 2].at[k2 % 2, k1]


def spread_out(kys):
    def find(refs, i, k3, k2, k1):
        if i == 0:
            return refs[k3].at[kys.index(k2)]
        if i == 1:
            return refs[4 + k3].at[k2, kys.index(k1)]
        return refs[8 + kys.index(k3)].at[k2]

    return find


def block_pieces(refs, piece, tile, column, ky, bits):
    low, high = bits
    rows = [pl.ds(first, count) for first, count in zip(FIRST, ROWS)]
    kz = [off.index(high * 2 + low) for off in Z_OFF]
    cols = column(ky, high)
    found = [(piece(refs, 0, kz[0], ky, None), tile.at[:, low, rows[0], cols])]
    for kx in range(4):
        found.append((piece(refs, 1, kx, kz[1], ky), tile.at[kx, low, rows[1], cols]))
    found.append((piece(refs, 2, ky, kz[2], None), tile.at[:, low, rows[2], cols]))
    return found


BITS = [(low, high) for low in range(2) for high in range(2)]


def route(ids_ref, mine_ref, gate_col, pick, put):
    before = lax.broadcasted_iota(jnp.int32, (128, 128), 0)
    before = (before < lax.broadcasted_iota(jnp.int32, (128, 128), 1)).astype(BF16)
    number = lax.broadcasted_iota(jnp.int32, (8, 32, 128), 1).astype(F32)
    line = lax.broadcasted_iota(jnp.int32, (8, 128), 0)

    def block(b, carry):
        mine = mine_ref[b].astype(F32)[0:8]
        routes = mine[:, 0:128]
        gates = mine[:, 128:256] + mine[:, 256:384] + mine[:, 384:512]
        named = jnp.zeros((8, 128), F32)
        weight = jnp.zeros((8, 128), F32)
        for e in range(8):
            hit = routes == ids_ref[e]
            any_hit = jnp.max(jnp.where(hit, 1.0, 0.0), axis=0, keepdims=True)
            gate = jnp.sum(jnp.where(hit, gates, 0.0), axis=0, keepdims=True)
            named = jnp.where(line == e, any_hit, named)
            weight = jnp.where(line == e, gate, weight)
        slot = jnp.dot(named.astype(BF16), before, preferred_element_type=F32)
        slot = jnp.where(named > 0, slot, -1.0)
        chosen = slot[:, None, :] == number
        one_hot = jnp.where(chosen, 1.0, 0.0).reshape(256, 128)
        pick[b] = one_hot.astype(BF16)
        put[b] = one_hot.T.astype(BF16)
        rows = pl.ds(pl.multiple_of(b * 32, 32), 32)
        gate_col[:, rows, :] = jnp.sum(
            jnp.where(chosen, weight[:, None, :], 0.0), axis=2, keepdims=True
        )
        return carry

    lax.fori_loop(0, 8, block, 0)


def y_pairs(outs, kys, n, cols_ref, tile):
    def column(ky, high):
        side = lax.rem(cols_ref[ky * 2 + high], 2)
        return pl.ds(pl.multiple_of(side * 512, 512), 512)

    find = spread_out(kys)
    return [
        pair for bits in BITS for pair in block_pieces(outs, find, tile, column, kys[n], bits)
    ]


def columns_of(cols_ref, ky):
    return pl.ds(pl.multiple_of(cols_ref[ky * 2] // 2 * 1024, 1024), 1024)


def expert_kernel(kys, ids_ref, cols_ref, mine_ref, wg, wu, wg2, wu2, wd, wd2, *rest):
    token_refs, rest = rest[:14], rest[14:]
    (h_ref, put), outs = rest[:2], rest[2:-8]
    tokens, sorted_rows, wbuf, act, gate_col, pick, t_sem, w_sem = rest[-8:]

    def load(ky):
        def column(ky, high):
            return pl.ds(pl.multiple_of(cols_ref[ky * 2 + high] * 512, 512), 512)

        pairs = [
            pair
            for bits in BITS
            for pair in block_pieces(token_refs, gathered, tokens, column, ky, bits)
        ]
        return [pltpu.make_async_copy(a, b, t_sem.at[ky, m]) for m, (a, b) in enumerate(pairs)]

    def fetch(ky):
        col, slot = columns_of(cols_ref, ky), ky % 2
        places = [(w, first, row) for first, pair in ((0, (wg, wu)), (4, (wg2, wu2)))
                  for row, w in zip((0, 192), pair)]
        return [
            pltpu.make_async_copy(
                w.at[:, :, col], wbuf.at[slot, pl.ds(first, 4), pl.ds(row, 192)], w_sem.at[slot, m]
            )
            for m, (w, first, row) in enumerate(places)
        ]

    def fetch_down(n):
        col = columns_of(cols_ref, kys[n])
        return [
            pltpu.make_async_copy(
                w.at[:, :, col],
                wbuf.at[0, pl.ds(first, 4), pl.ds(n * 192, 192)],
                w_sem.at[0, n * 2 + m],
            )
            for m, (w, first) in enumerate(((wd, 0), (wd2, 4)))
        ]

    def start(copies):
        for copy in copies:
            copy.start()

    def finish(copies):
        for copy in copies:
            copy.wait()

    for ky in range(2):
        start(load(ky))
        start(fetch(ky))
    route(ids_ref, mine_ref, gate_col, pick, put)
    for ky in range(4):
        finish(load(ky))
        if ky < 2:
            start(load(ky + 2))
        col = columns_of(cols_ref, ky)

        def dispatch(b, carry):
            rows = jnp.dot(
                pick[b], tokens[b // 2, lax.rem(b, 2), :, col], preferred_element_type=F32
            )
            rows = rows.astype(BF16).reshape(4, 2, 32, 1024)
            sorted_rows[:, :, pl.ds(pl.multiple_of(b * 32, 32), 32)] = rows
            return carry

        lax.fori_loop(0, 8, dispatch, 0, unroll=8)
        finish(fetch(ky))

        def project(e, carry):
            part = lax.dot_general(
                sorted_rows[e // 2, lax.rem(e, 2)],
                wbuf[ky % 2, e],
                (((1,), (1,)), ((), ())),
                preferred_element_type=F32,
            )
            if ky > 0:
                part = act[e] + part
            if ky < 3:
                act[e] = part
            else:
                gate, up = part[:, :192], part[:, 192:]
                h_ref[e] = (gate / (1.0 + jnp.exp(-gate)) * up * gate_col[e]).astype(BF16)
            return carry

        lax.fori_loop(0, 8, project, 0, unroll=8)
        if ky < 2:
            start(fetch(ky + 2))
        if ky == 2:
            start(fetch_down(0) + fetch_down(1))
    stores = []
    for n in range(2):
        finish(fetch_down(n))

        def project_out(e, carry):
            down = wbuf[0, e, pl.ds(n * 192, 192)]
            out = jnp.dot(h_ref[e], down, preferred_element_type=F32)
            rows = pl.ds(pl.multiple_of(e * 32, 32), 32)
            sorted_rows[:, :, rows] = out.astype(BF16).reshape(4, 2, 32, 1024)
            return carry

        lax.fori_loop(0, 8, project_out, 0, unroll=8)
        col = pl.ds(1024 * n, 1024)

        def combine(b, carry):
            at = b // 2, lax.rem(b, 2)
            out = jnp.dot(put[b], sorted_rows[at[0], at[1]], preferred_element_type=F32)
            tokens[at[0], at[1], :, col] = out.astype(BF16)
            return carry

        lax.fori_loop(0, 8, combine, 0, unroll=8)
        pairs = y_pairs(outs, kys, n, cols_ref, tokens.at[:, :, :, col])
        stores.append(
            [pltpu.make_async_copy(b, a, t_sem.at[n, m]) for m, (a, b) in enumerate(pairs)]
        )
        start(stores[n])
    finish(stores[0] + stores[1])


def down_kernel(kys, cols_ref, h_ref, put_ref, wd, wd2, *rest):
    outs = rest[:-7]
    h, put, wbuf, expert_rows, ybuf, w_sem, y_sem = rest[-7:]

    def fetch(n):
        col = columns_of(cols_ref, kys[n])
        return [
            pltpu.make_async_copy(wd.at[:, :, col], wbuf.at[n, pl.ds(0, 4)], w_sem.at[n, 0]),
            pltpu.make_async_copy(wd2.at[:, :, col], wbuf.at[n, pl.ds(4, 4)], w_sem.at[n, 1]),
        ]

    def stores(n):
        pairs = y_pairs(outs, kys, n, cols_ref, ybuf.at[n])
        return [pltpu.make_async_copy(b, a, y_sem.at[n, m]) for m, (a, b) in enumerate(pairs)]

    inputs = [
        pltpu.make_async_copy(h_ref, h, w_sem.at[2, 0]),
        pltpu.make_async_copy(put_ref, put, w_sem.at[2, 1]),
    ]
    for copy in inputs + fetch(0) + fetch(1):
        copy.start()
    for copy in inputs:
        copy.wait()
    for n in range(2):
        for copy in fetch(n):
            copy.wait()

        def project(e, carry):
            out = jnp.dot(h[e], wbuf[n, e], preferred_element_type=F32)
            rows = pl.ds(pl.multiple_of(e * 32, 32), 32)
            expert_rows[:, rows] = out.astype(BF16).reshape(8, 32, 1024)
            return carry

        lax.fori_loop(0, 8, project, 0, unroll=4)

        def combine(b, carry):
            out = jnp.dot(put[b], expert_rows[b], preferred_element_type=F32)
            ybuf[n, b // 2, lax.rem(b, 2)] = out.astype(BF16)
            return carry

        lax.fori_loop(0, 8, combine, 0, unroll=8)
        for copy in stores(n):
            copy.start()
    for n in range(2):
        for copy in stores(n):
            copy.wait()


def local(tokens, routes, gates, w_gate, w_up, w_down):
    e, t = lax.axis_index("expert"), lax.axis_index("tensor")
    y, zhi = t // 2, t % 2
    ids = jnp.concatenate([e * 4 + jnp.arange(4), (e ^ 1) * 4 + jnp.arange(4)]).astype(F32)
    cols = jnp.stack([(y ^ OFF[ky]) * 2 + (zhi ^ high) for ky in range(4) for high in range(2)])
    cols = cols.astype(jnp.int32)

    top = lax.reduce_precision(gates, 8, 7)
    rest = gates - top
    middle = lax.reduce_precision(rest, 8, 7)
    packed = jnp.concatenate([part.T for part in (routes.astype(F32), top, middle, rest - middle)], 1)
    packed = jnp.pad(packed.astype(BF16), ((0, 8), (0, 0)))

    wg2 = from_other_core(w_gate)
    along_x = join(tokens[:48], tokens[96:], packed)[None]
    along_y = tokens[48:96][None]
    for mask in (1, 3):
        got = swap(along_x, 0, mask), swap(along_y, 1, mask)
        along_x, along_y = join(along_x, got[0]), join(along_y, got[1])
    along_x, along_y, wg2, w_up = lax.optimization_barrier((along_x, along_y, wg2, w_up))
    wu2 = from_other_core(w_up)
    parts = [along_x[:, :48], along_y, along_x[:, 48:]]
    parts = [join(p, swap(p, MIDDLE[i], MASKS[i][0])) for i, p in enumerate(parts)]
    mine = parts[2][:, 32:].reshape(2, 4, 16, 512)
    mine = jnp.swapaxes(mine, 0, 1).reshape(8, 16, 512)
    parts[2] = parts[2][:, :32]
    parts, wu2, w_down, mine, ids, cols = lax.optimization_barrier(
        (parts, wu2, w_down, mine, ids, cols)
    )
    wd2 = from_other_core(w_down)
    parts = [join(p, swap(p, MIDDLE[i], MASKS[i][1])) for i, p in enumerate(parts)]
    parts, wd2 = lax.optimization_barrier((parts, wd2))
    parts = gather_last(parts)
    pieces = [p.reshape(p.shape[0] // 4, 4, p.shape[1], 512) for p in parts]
    smem = pl.BlockSpec(memory_space=pltpu.SMEM)
    vmem = pl.BlockSpec(memory_space=pltpu.VMEM)
    hbm = pl.BlockSpec(memory_space=pl.ANY)
    shapes = [(2, 4, ROWS[0], 512)] * 4 + [(4, 2, ROWS[1], 512)] * 4
    shapes = [
        jax.ShapeDtypeStruct(shape, BF16) for shape in shapes + [(4, 4, ROWS[2], 512)] * 2
    ]
    hidden, put, *first = pl.pallas_call(
        functools.partial(expert_kernel, (2, 3)),
        out_shape=[
            jax.ShapeDtypeStruct((8, 256, 192), BF16),
            jax.ShapeDtypeStruct((8, 128, 256), BF16),
        ]
        + shapes,
        in_specs=[smem, smem, vmem] + [hbm] * 20,
        out_specs=[vmem, vmem] + [hbm] * 10,
        scratch_shapes=[
            pltpu.VMEM((4, 2, 128, 4096), BF16),
            pltpu.VMEM((4, 2, 256, 1024), BF16),
            pltpu.VMEM((2, 8, 384, 1024), BF16),
            pltpu.VMEM((8, 256, 384), F32),
            pltpu.VMEM((8, 256, 1), F32),
            pltpu.VMEM((8, 256, 128), BF16),
            pltpu.SemaphoreType.DMA((4, 24)),
            pltpu.SemaphoreType.DMA((2, 4)),
        ],
        compiler_params=pltpu.CompilerParams(vmem_limit_bytes=VMEM_EXPERTS),
        cost_estimate=pl.CostEstimate(
            flops=20 * 10**9, bytes_accessed=50 * 10**6, transcendentals=0
        ),
        name="experts",
    )(ids, cols, mine, w_gate, w_up, wg2, wu2, w_down, wd2, *pieces)

    second = pl.pallas_call(
        functools.partial(down_kernel, (0, 1)),
        out_shape=shapes,
        in_specs=[smem] + [hbm] * 4,
        out_specs=[hbm] * 10,
        scratch_shapes=[
            pltpu.VMEM((8, 256, 192), BF16),
            pltpu.VMEM((8, 128, 256), BF16),
            pltpu.VMEM((2, 8, 192, 1024), BF16),
            pltpu.VMEM((8, 256, 1024), BF16),
            pltpu.VMEM((2, 4, 2, 128, 1024), BF16),
            pltpu.SemaphoreType.DMA((3, 2)),
            pltpu.SemaphoreType.DMA((2, 24)),
        ],
        compiler_params=pltpu.CompilerParams(vmem_limit_bytes=50 * 2**20),
        cost_estimate=pl.CostEstimate(
            flops=6 * 10**9, bytes_accessed=12 * 10**6, transcendentals=0
        ),
        name="down",
    )(cols, hidden, put, w_down, wd2)
    return scatter_sums(first, second)


def solution(mesh):
    placed = (
        P("expert", "tensor"),
        P("expert", None),
        P("expert", None),
        P("expert", "tensor", None),
        P("expert", "tensor", None),
        P("expert", "tensor", None),
    )
    return jax.shard_map(
        local, mesh=mesh, in_specs=placed, out_specs=P("expert", "tensor"), check_vma=False
    )
```
